32 devices in a mesh: gx: 4 (over z), gy: 2 (over y), gz: 4 (over x, core).
Axes of the slice: x: 2, y: 2, z: 4, core: 2. Of those that a mesh axis runs over, the one named last changes fastest.
Arguments:
- orbitals: float32 [2, 64, 32, 512], P(None, 'gx', 'gy', 'gz'), may hold values from -6 to 6
- potential: float32 [64, 32, 512], P('gx', 'gy', 'gz'), may hold values from -2 to 1
- projectors: float32 [4, 2, 4, 8, 4, 4, 4096], P('gx', 'gy', 'gz'), as said below
- coupling: float32 [4, 2, 4, 8, 4, 4, 4], P('gx', 'gy', 'gz'), as said below
- block_starts: int32 [4, 2, 4, 8, 4, 3], P('gx', 'gy', 'gz'), may hold values from 0 to 127, as said below
- owner_counts: int32 [4, 2, 4, 8], P('gx', 'gy', 'gz'), may hold values from 1 to 4, as said below
Outputs:
- applied: float32 [2, 64, 32, 512], P(None, 'gx', 'gy', 'gz')
The draws below stay inside these ranges and needn't reach their ends.
Inputs may be any that keep to these rules, and one draw needn't show every extreme that they name: `block_starts`: entry [q, o, s, d] is the start along dimension d, inside its owner box, of the block of slot s of the box q - o (periodically, o = (a, b, c) with c fastest); it is below 16, 16, 128 for d = 0, 1, 2, and all eight copies of an atom agree. `owner_counts`: entry [q, o] is the number of live slots of the box q - o (periodically, o ordered as in block_starts); the eight copies agree. `projectors`: the eight copies of an atom's values agree. `coupling`: the eight copies of an atom's matrix agree.
All inputs are finite; a program needn't handle non-finite values.
Results may differ from the reference program's by a relative error of at most 0.00005.
Values sent between devices are 32-bit elements; how exact they have to be, the bound alone decides.
A program may use at most 64 MiB of HBM per device.

```python
import jax
import jax.numpy as jnp
from jax import lax

CX = 16
CY = 16
CZ = 128
BANDS = 2
PB = 16
NPROJ = 4
SLOTS = 4
NX = 64
NY = 32
NZ = 512
N_GX = 4
N_GY = 2
N_GZ = 4


def spread(owner):
    copies = []
    for shift_a in (0, 1):
        for shift_b in (0, 1):
            for shift_c in (0, 1):
                copies.append(jnp.roll(owner, (shift_a, shift_b, shift_c), axis=(0, 1, 2)))
    return jnp.stack(copies, axis=3)


def draw_block_starts(key, part):
    key = jax.random.fold_in(key, 11)
    keys = jax.random.split(key, 3)
    shape = (N_GX, N_GY, N_GZ, SLOTS)
    start_x = jax.random.randint(keys[0], shape, 0, CX)
    start_y = jax.random.randint(keys[1], shape, 0, CY)
    start_z = jax.random.randint(keys[2], shape, 0, CZ)
    owner = jnp.stack([start_x, start_y, start_z], axis=-1).astype(jnp.int32)
    owner = owner.at[0, 0, 0, 0].set(jnp.array([CX - 1, CY - 1, CZ - 1], jnp.int32))
    owner = owner.at[0, 0, 0, 1].set(jnp.zeros((3,), jnp.int32))
    return spread(owner)


def draw_owner_counts(key, part):
    key = jax.random.fold_in(key, 17)
    owner = jax.random.randint(key, (N_GX, N_GY, N_GZ), 1, SLOTS + 1).astype(jnp.int32)
    owner = owner.at[0, 0, 0].set(SLOTS)
    return spread(owner)


def draw_projectors(key, part):
    key = jax.random.fold_in(key, 23)
    keys = jax.random.split(key, 1)
    shape = (N_GX, N_GY, N_GZ, SLOTS, NPROJ, PB ** 3)
    owner = jax.random.normal(keys[0], shape, jnp.float32) * 0.125
    return spread(owner)


def draw_coupling(key, part):
    key = jax.random.fold_in(key, 31)
    keys = jax.random.split(key, 2)
    shape = (N_GX, N_GY, N_GZ, SLOTS, NPROJ, NPROJ)
    diag = jax.random.uniform(keys[0], shape[:5], jnp.float32, 0.5, 2.0)
    off = jax.random.normal(keys[1], shape, jnp.float32) * 0.25
    off = 0.5 * (off + jnp.swapaxes(off, -1, -2))
    unit = jnp.eye(NPROJ, dtype=jnp.float32)
    owner = off * (1.0 - unit) + diag[..., None] * unit
    return spread(owner)


def block_scale(own_key, dims, cuts, least, largest):
    def one(axis_at, shards_of):
        steps = jax.random.uniform(jax.random.fold_in(jax.random.fold_in(own_key, 6), axis_at), (shards_of,), jnp.float32, least / len(cuts), largest / len(cuts))
        return jnp.repeat(jnp.exp(steps), dims[axis_at] // shards_of).reshape((-1,) + (1,) * (len(dims) - axis_at - 1))

    gain = one(*cuts[0])
    for cut in cuts[1:]:
        gain = gain * one(*cut)
    return gain


def bell_draw(rng, extent, width, most, cuts=(), held_as=jnp.bfloat16):
    drawn = width * jax.random.normal(rng, extent, jnp.float32)
    if cuts:
        drawn = drawn * block_scale(rng, extent, cuts, -0.22, 0.18)
    return jnp.clip(drawn, -most, most).astype(held_as)


def setup_inputs(seed: int = 0) -> dict:
    key_list = jax.random.split(jax.random.key(seed), 7)
    orbitals = bell_draw(key_list[0], (BANDS, NX, NY, NZ), 1.0, 6.0, ((1, 4), (2, 2), (3, 4)), jnp.float32)
    potential = jnp.clip(-2.0 + 3.0 * jax.random.uniform(key_list[1], (NX, NY, NZ), jnp.float32) ** block_scale(key_list[1], (NX, NY, NZ), ((0, 4), (1, 2), (2, 4)), -0.2, 0.2), -2.0, 1.0)
    projectors = draw_projectors(jax.random.fold_in(key_list[6], 71), 0)
    coupling = draw_coupling(jax.random.fold_in(key_list[6], 71), 0)
    block_starts = draw_block_starts(jax.random.fold_in(key_list[6], 71), 0)
    owner_counts = draw_owner_counts(jax.random.fold_in(key_list[6], 71), 0)
    return dict(orbitals=orbitals, potential=potential, projectors=projectors, coupling=coupling, block_starts=block_starts, owner_counts=owner_counts)


COEFF = [-5369.0 / 1800.0, 12.0 / 7.0, -15.0 / 56.0, 10.0 / 189.0, -1.0 / 112.0, 2.0 / 1925.0, -1.0 / 16632.0]


def laplace(field):
    total = 3.0 * COEFF[0] * field
    for axis_id in (1, 2, 3):
        for step in range(1, 7):
            total = total + COEFF[step] * (jnp.roll(field, step, axis_id) + jnp.roll(field, -step, axis_id))
    return total


def reference(orbitals, potential, projectors, coupling, block_starts, owner_counts):
    bands = orbitals.shape[0]
    boxes_x, boxes_y, boxes_z = block_starts.shape[0], block_starts.shape[1], block_starts.shape[2]
    starts = block_starts[:, :, :, 0]
    base_x = (jnp.arange(boxes_x, dtype=jnp.int32) * CX)[:, None, None, None]
    base_y = (jnp.arange(boxes_y, dtype=jnp.int32) * CY)[None, :, None, None]
    base_z = (jnp.arange(boxes_z, dtype=jnp.int32) * CZ)[None, None, :, None]
    glob_x = (base_x + starts[..., 0]).reshape(-1)
    glob_y = (base_y + starts[..., 1]).reshape(-1)
    glob_z = (base_z + starts[..., 2]).reshape(-1)
    span = jnp.arange(PB, dtype=jnp.int32)
    index_x = ((glob_x[:, None] + span[None, :]) % NX)[:, :, None, None]
    index_y = ((glob_y[:, None] + span[None, :]) % NY)[:, None, :, None]
    index_z = ((glob_z[:, None] + span[None, :]) % NZ)[:, None, None, :]
    blocks = orbitals[:, index_x, index_y, index_z].reshape(bands, -1, PB ** 3)
    values = projectors[:, :, :, 0].reshape(-1, NPROJ, PB ** 3)
    coefficients = jnp.einsum('bkc,kjc->kbj', blocks, values, precision=lax.Precision.HIGHEST)
    slot_ids = jnp.arange(SLOTS, dtype=jnp.int32)
    live = (slot_ids[None, :] < owner_counts[:, :, :, 0].reshape(-1, 1)).astype(jnp.float32).reshape(-1)
    matrices = coupling[:, :, :, 0].reshape(-1, NPROJ, NPROJ)
    weighted = jnp.einsum('kij,kbj->kbi', matrices, coefficients, precision=lax.Precision.HIGHEST) * live[:, None, None]
    contrib = jnp.einsum('kbj,kjc->bkc', weighted, values, precision=lax.Precision.HIGHEST)
    contrib = contrib.reshape(bands, -1, PB, PB, PB)
    nonlocal_part = jnp.zeros_like(orbitals).at[:, index_x, index_y, index_z].add(contrib)
    return -0.5 * laplace(orbitals) + potential[None] * orbitals + nonlocal_part
```

```python
import functools

import jax
import jax.numpy as jnp
from jax import lax
from jax.experimental import pallas as pl
from jax.experimental.pallas import tpu as pltpu
from jax.sharding import PartitionSpec as P

MESH = pl.DeviceIdType.MESH
HI = lax.Precision.HIGHEST
F32 = jnp.float32
COEFF = [
    -5369.0 / 1800.0,
    12.0 / 7.0,
    -15.0 / 56.0,
    10.0 / 189.0,
    -1.0 / 112.0,
    2.0 / 1925.0,
    -1.0 / 16632.0,
]
PAD = 40


def iota(shape, dim):
    return lax.broadcasted_iota(jnp.int32, shape, dim)


def band(distance):
    d = jnp.abs(distance)
    out = jnp.zeros(distance.shape, F32)
    for k in range(1, 7):
        out = jnp.where(d == k, -0.5 * COEFF[k], out)
    return out


def shear(v, back):
    axis = v.ndim - 1
    sub = iota(v.shape, axis - 1)
    for bit in (1, 2, 4):
        turn = (128 - 16 * bit) if back else 16 * bit
        v = jnp.where((sub & bit) != 0, pltpu.roll(v, turn, axis), v)
    return v


def residues(n):
    return [0, 1] if n == 2 else [0, 1, n - 1]


def kernel(
    sizes,
    x_hbm, pot_hbm, p_hbm, cpl_ref, st_ref, cnt_ref,
    out_ref,
    xpad, xe, ye, pot, pv, pr, sheared, accs, zs, zr, recv, zc, wrep, cs, mprime,
    lsem, hsend, hrecv, psend, precv,
):
    names = ("gx", "gy", "gz")
    me = [lax.axis_index(name) for name in names]
    res = [residues(n) for n in sizes]
    slots = {}
    for ex in res[0]:
        for ey in res[1]:
            for ez in res[2]:
                slots[(ex, ey, ez)] = len(slots)

    def device(offset):
        return tuple(lax.rem(me[d] + offset[d] % sizes[d], sizes[d]) for d in range(3))

    def slot_of(offset):
        return slots[tuple(offset[d] % sizes[d] for d in range(3))]

    load_x = pltpu.make_async_copy(x_hbm, xe.at[:, 6:22], lsem.at[0])
    load_y = pltpu.make_async_copy(x_hbm, ye.at[:, :, 8:24], lsem.at[1])
    load_p = pltpu.make_async_copy(p_hbm, pv, lsem.at[2])
    load_pot = pltpu.make_async_copy(pot_hbm, pot, lsem.at[3])
    load_x.start()
    load_p.start()
    load_y.start()
    load_pot.start()

    barrier = pltpu.get_barrier_semaphore()
    others = [e for e in slots if e != (0, 0, 0)]
    for e in others:
        pl.semaphore_signal(barrier, inc=1, device_id=device(e), device_id_type=MESH)

    def clear(i, carry):
        for b in range(2):
            xpad[b, i] = jnp.zeros((48, 128), F32)
        return carry

    lax.fori_loop(0, 48, clear, 0)
    for b in range(2):
        zc[b] = jnp.zeros((112, 128), F32)

    for s in range(4):
        for i in range(4):
            cs[pl.ds((s * 4 + i) * 4, 4), :] = cpl_ref[s, i]
    pick = (iota((256, 8), 0) // 32 == iota((256, 8), 1)).astype(F32)
    per_row = lax.dot_general(pick, cs[...], (((1,), (1,)), ((), ())), precision=HI,
                              preferred_element_type=F32)
    r64, c64 = iota((256, 64), 0), iota((256, 64), 1)
    own = ((r64 // 8) % 4 == c64 // 16) & (r64 % 4 == (c64 // 4) % 4)
    per_row = jnp.where(own, per_row, 0.0)
    spread = (iota((64, 256), 0) % 4 == iota((64, 256), 1) % 4).astype(F32)
    wide = lax.dot_general(per_row, spread, (((1,), (0,)), ((), ())), precision=HI,
                           preferred_element_type=F32)
    same = iota((256, 256), 0) // 4 == iota((256, 256), 1) // 4
    mprime[...] = jnp.where(same, wide, 0.0)

    pl.semaphore_wait(barrier, len(others))

    sends = []

    def send(src, dst, k, offset):
        copy = pltpu.make_async_remote_copy(
            src_ref=src, dst_ref=dst, send_sem=hsend.at[k], recv_sem=hrecv.at[k],
            device_id=device(offset), device_id_type=MESH,
        )
        copy.start()
        sends.append(copy)

    send(x_hbm.at[:, :, 8:16, :], ye.at[:, :, 0:8, :], 0, (0, 1, 0))
    send(x_hbm.at[:, :, 0:8, :], ye.at[:, :, 24:32, :], 1, (0, -1, 0))
    send(x_hbm.at[:, 10:16], xe.at[:, 0:6], 2, (1, 0, 0))
    send(x_hbm.at[:, 0:6], xe.at[:, 22:28], 3, (-1, 0, 0))

    load_x.wait()

    def lay(x, carry):
        for b in range(2):
            xpad[b, 16 + x, 16:32, :] = shear(xe[b, 6 + x], False)
            sheared[b, x] = jnp.zeros((16, 128), F32)
        return carry

    lax.fori_loop(0, 16, lay, 0)
    flat = xe[:, 6:22].reshape(512, 128)
    row, col = iota((16, 128), 0), iota((16, 128), 1)
    sel = (col == jnp.where(row < 8, 120 + row, row - 8)).astype(F32)
    zs[...] = lax.dot_general(sel, flat, (((1,), (1,)), ((), ())), precision=HI,
                              preferred_element_type=F32)
    send(zs.at[0:8], zr.at[0:8], 4, (0, 0, 1))
    send(zs.at[8:16], zr.at[8:16], 5, (0, 0, -1))
    load_p.wait()

    lane, sub = iota((8, 128), 1), iota((8, 128), 0)

    def place(n):
        o, s = n >> 2, n & 3
        a = st_ref[0, s, o] - 16 * (o >> 2)
        b0 = st_ref[1, s, o] - 16 * ((o >> 1) & 1)
        c = st_ref[2, s, o] - 128 * (o & 1)
        return o, s, a, b0, c

    def turn(n, carry):
        _, _, _, b0, c = place(n)
        by = (c + 16 * b0) & 127
        for i in range(4):
            plane = pv[pl.ds(n * 128 + i, 32, stride=4), :]
            pr[pl.ds(n * 128 + i * 32, 32), :] = pltpu.roll(plane, by, 1)
        return carry

    lax.fori_loop(0, 32, turn, 0)

    def gather(n, carry):
        _, _, a, b0, c = place(n)
        z = (lane - 16 * (sub + b0)) & 127
        keep = (z >= c) & (z < c + 16)
        acc = [jnp.zeros((8, 128), F32) for _ in range(8)]
        for x in range(16):
            for yh in range(2):
                rows = [
                    jnp.broadcast_to(pr[pl.ds(n * 128 + i * 32 + x * 2 + yh, 1), :], (8, 128))
                    for i in range(4)
                ]
                for b in range(2):
                    g = xpad[b, 16 + a + x, pl.ds(16 + b0 + 8 * yh, 8), :]
                    g = jnp.where(keep, g, 0.0)
                    for i in range(4):
                        acc[b * 4 + i] = acc[b * 4 + i] + g * rows[i]
        for k in range(8):
            accs[pl.ds(n * 64 + k * 8, 8), :] = acc[k]
        return carry

    lax.fori_loop(0, 32, gather, 0)

    total = accs[pl.ds(0, 256, stride=8), :]
    for k in range(1, 8):
        total = total + accs[pl.ds(k, 256, stride=8), :]
    mine = lax.dot_general(jnp.ones((8, 128), F32), total, (((1,), (1,)), ((), ())),
                           precision=HI, preferred_element_type=F32)
    recv[0] = mine[0:1]
    parts = []
    for k, e in enumerate(others):
        copy = pltpu.make_async_remote_copy(
            src_ref=recv.at[0], dst_ref=recv.at[slot_of(tuple(-v for v in e))],
            send_sem=psend.at[k], recv_sem=precv.at[slot_of(tuple(-v for v in e))],
            device_id=device(e), device_id_type=MESH,
        )
        copy.start()
        parts.append(copy)

    load_y.wait()
    load_pot.wait()
    r128, c128 = iota((128, 128), 0), iota((128, 128), 1)
    near = jnp.where(r128 == c128, -0.5 * 3.0 * COEFF[0], band(r128 - c128))
    out_ref[...] = lax.dot_general(flat, near, (((1,), (0,)), ((), ())), precision=HI,
                                   preferred_element_type=F32).reshape(2, 16, 16, 128)
    for copy in sends:
        copy.wait()
    far = band(jnp.where(row < 8, row - 8, 120 + row) - col)
    edge = lax.dot_general(zr[...], far, (((0,), (0,)), ((), ())), precision=HI,
                           preferred_element_type=F32).reshape(2, 16, 16, 128)
    out_ref[...] += edge

    def stencil(x, carry):
        for b in range(2):
            acc = pot[x] * xe[b, x + 6] + out_ref[b, x]
            for k in range(1, 7):
                four = (ye[b, x, 8 - k : 24 - k, :] + ye[b, x, 8 + k : 24 + k, :]) + (
                    xe[b, x + 6 - k] + xe[b, x + 6 + k]
                )
                acc = acc + (-0.5 * COEFF[k]) * four
            out_ref[b, x] = acc
        return carry

    lax.fori_loop(0, 16, stencil, 0)

    for copy in parts:
        copy.wait()

    def got(dx, dy, dz):
        r = recv[slot_of((dx, dy, dz))]
        return r[:, 0:128], r[:, 128:256]

    lane1 = iota((1, 128), 1)
    upper_y, upper_z = (lane1 & 64) != 0, (lane1 & 32) != 0
    halves = []
    for h in range(2):
        by_z = {}
        for dz in (-1, 0, 1):
            by_y = {}
            for dy in (-1, 0, 1):
                by_y[dy] = got(0, dy, dz)[h] + got(1 - 2 * h, dy, dz)[1 - h]
            crossed = jnp.where(upper_y, by_y[1], by_y[-1])
            by_z[dz] = by_y[0] + pltpu.roll(crossed, 64, 1)
        down = pltpu.roll(by_z[1], 96, 1)
        up = pltpu.roll(by_z[-1], 32, 1)
        halves.append(by_z[0] + jnp.where(upper_z, up, down))
    sums = jnp.concatenate(halves, axis=1)
    wrep[...] = lax.dot_general(mprime[...] * sums, jnp.ones((256, 128), F32),
                                (((1,), (0,)), ((), ())), precision=HI,
                                preferred_element_type=F32)

    def scatter(n, carry):
        o, s, a, b0, c = place(n)
        live = jnp.where(s < cnt_ref[o], 1.0, 0.0).astype(F32)
        planes = [pr[pl.ds(n * 128 + i * 32, 32), :] for i in range(4)]
        for b in range(2):
            mix = jnp.zeros((32, 128), F32)
            for i in range(4):
                mix = mix + planes[i] * (wrep[pl.ds(n * 8 + b * 4 + i, 1), :] * live)
            zc[b, PAD : PAD + 32, :] = mix
        low = b0 >> 3
        rest = b0 & 7
        first = sub >= rest
        z = (lane - 16 * sub) & 127
        window = (z >= c) & (z < c + 16)
        for t in range(2):
            y = 8 * t + sub - b0
            keep = window & (y >= 0) & (y < 16)
            start = PAD - 2 * a + t - low
            for x in range(16):
                for b in range(2):
                    one = jnp.broadcast_to(zc[b, pl.ds(start + 2 * x, 1), :], (8, 128))
                    two = jnp.broadcast_to(zc[b, pl.ds(start + 2 * x - 1, 1), :], (8, 128))
                    v = jnp.where(first, one, two)
                    sheared[b, x, 8 * t : 8 * t + 8, :] += jnp.where(keep, v, 0.0)
        return carry

    lax.fori_loop(0, 32, scatter, 0)

    def finish(x, carry):
        for b in range(2):
            out_ref[b, x] += shear(sheared[b, x], True)
        return carry

    lax.fori_loop(0, 16, finish, 0)


def solution(mesh):
    sizes = tuple(mesh.shape[name] for name in ("gx", "gy", "gz"))
    nslots = 1
    for n in sizes:
        nslots *= len(residues(n))

    def on_device(orbitals, potential, projectors, coupling, block_starts, owner_counts):
        rows = projectors.reshape(32, 4, 32, 128).transpose(0, 2, 1, 3).reshape(4096, 128)
        matrices = coupling.reshape(8, 4, 4, 4).transpose(1, 2, 3, 0)
        starts = block_starts.reshape(8, 4, 3).transpose(2, 1, 0)
        counts = owner_counts.reshape(8)
        anyspace = pl.BlockSpec(memory_space=pl.ANY)
        vmem = pl.BlockSpec(memory_space=pltpu.VMEM)
        smem = pl.BlockSpec(memory_space=pltpu.SMEM)
        return pl.pallas_call(
            functools.partial(kernel, sizes),
            out_shape=jax.ShapeDtypeStruct((2, 16, 16, 128), F32),
            in_specs=[anyspace, anyspace, anyspace, vmem, smem, smem],
            out_specs=vmem,
            scratch_shapes=[
                pltpu.VMEM((2, 48, 48, 128), F32),
                pltpu.VMEM((2, 28, 16, 128), F32),
                pltpu.VMEM((2, 16, 32, 128), F32),
                pltpu.VMEM((16, 16, 128), F32),
                pltpu.VMEM((4096, 128), F32),
                pltpu.VMEM((4096, 128), F32),
                pltpu.VMEM((2, 16, 16, 128), F32),
                pltpu.VMEM((2048, 128), F32),
                pltpu.VMEM((16, 512), F32),
                pltpu.VMEM((16, 512), F32),
                pltpu.VMEM((nslots, 1, 256), F32),
                pltpu.VMEM((2, 112, 128), F32),
                pltpu.VMEM((256, 128), F32),
                pltpu.VMEM((64, 8), F32),
                pltpu.VMEM((256, 256), F32),
                pltpu.SemaphoreType.DMA((4,)),
                pltpu.SemaphoreType.DMA((6,)),
                pltpu.SemaphoreType.DMA((6,)),
                pltpu.SemaphoreType.DMA((nslots,)),
                pltpu.SemaphoreType.DMA((nslots,)),
            ],
            compiler_params=pltpu.CompilerParams(
                collective_id=0, has_side_effects=True, vmem_limit_bytes=32 * 1024 * 1024
            ),
        )(orbitals, potential, rows, matrices, starts, counts)

    in_specs = (
        P(None, "gx", "gy", "gz"),
        P("gx", "gy", "gz"),
        P("gx", "gy", "gz", None, None, None, None),
        P("gx", "gy", "gz", None, None, None, None),
        P("gx", "gy", "gz", None, None, None),
        P("gx", "gy", "gz", None),
    )
    return jax.shard_map(
        on_device, mesh=mesh, in_specs=in_specs,
        out_specs=P(None, "gx", "gy", "gz"), check_vma=False,
    )
```

```python
import functools

import jax
import jax.numpy as jnp
from jax import lax
from jax.experimental import pallas as pl
from jax.experimental.pallas import tpu as pltpu
from jax.sharding import PartitionSpec as P

MESH = pl.DeviceIdType.MESH
HI = lax.Precision.HIGHEST
F32 = jnp.float32
COEFF = [
    -5369.0 / 1800.0,
    12.0 / 7.0,
    -15.0 / 56.0,
    10.0 / 189.0,
    -1.0 / 112.0,
    2.0 / 1925.0,
    -1.0 / 16632.0,
]


def iota(shape, dim):
    return lax.broadcasted_iota(jnp.int32, shape, dim)


def band(distance):
    d = jnp.abs(distance)
    out = jnp.zeros(distance.shape, F32)
    for k in range(1, 7):
        out = jnp.where(d == k, -0.5 * COEFF[k], out)
    return out


def residues(n):
    return [0, 1] if n == 2 else [0, 1, n - 1]


def kernel(
    sizes,
    x_hbm, pot_hbm, p_hbm, cpl_hbm, st_hbm, cnt_hbm,
    out_ref,
    xt, xe, ye, pot, pv, pr, sheared, accs, zs, zr, recv, zc, wrep, cs, mprime, fold,
    cpl_ref, st_ref, cnt_ref,
    lsem, hsend, hrecv, psend, precv,
):
    names = ("gx", "gy", "gz")
    me = [lax.axis_index(name) for name in names]
    res = [residues(n) for n in sizes]
    slots = {}
    for ex in res[0]:
        for ey in res[1]:
            for ez in res[2]:
                slots[(ex, ey, ez)] = len(slots)

    def device(offset):
        return tuple(lax.rem(me[d] + offset[d] % sizes[d], sizes[d]) for d in range(3))

    def slot_of(offset):
        return slots[tuple(offset[d] % sizes[d] for d in range(3))]

    load_x = pltpu.make_async_copy(x_hbm, xe.at[:, 6:22], lsem.at[0])
    load_y = pltpu.make_async_copy(x_hbm, ye.at[:, :, 8:24], lsem.at[1])
    load_p = pltpu.make_async_copy(p_hbm, pv, lsem.at[2])
    load_pot = pltpu.make_async_copy(pot_hbm, pot, lsem.at[3])
    load_st = pltpu.make_async_copy(st_hbm, st_ref, lsem.at[4])
    load_cnt = pltpu.make_async_copy(cnt_hbm, cnt_ref, lsem.at[5])
    load_cpl = pltpu.make_async_copy(cpl_hbm, cpl_ref, lsem.at[6])
    load_st.start()
    load_p.start()
    load_x.start()
    load_cpl.start()
    load_cnt.start()
    load_y.start()
    load_pot.start()

    barrier = pltpu.get_barrier_semaphore()
    others = [e for e in slots if e != (0, 0, 0)]
    for e in others:
        pl.semaphore_signal(barrier, inc=1, device_id=device(e), device_id_type=MESH)

    def clear(i, carry):
        for b in range(2):
            xt[b, i] = jnp.zeros((48, 128), F32)
        return carry

    lax.fori_loop(0, 48, clear, 0)

    def clear_mix(i, carry):
        zc[i] = jnp.zeros((48, 128), F32)
        return carry

    lax.fori_loop(0, 48, clear_mix, 0)

    def clear_sum(i, carry):
        for b in range(2):
            sheared[b, i] = jnp.zeros((16, 128), F32)
        return carry

    lax.fori_loop(0, 16, clear_sum, 0)

    lane = iota((8, 128), 1)

    def place(o, s):
        a = st_ref[0, s, o] - 16 * (o >> 2)
        b0 = st_ref[1, s, o] - 16 * ((o >> 1) & 1)
        c = st_ref[2, s, o] - 128 * (o & 1)
        return a, b0, c

    load_st.wait()
    load_cnt.wait()
    load_p.wait()

    def turn(o, carry):
        for s in range(4):
            n = o * 4 + s
            _, b0, c = place(o, s)
            by = (c + 16 * b0) & 127
            for i in range(4):
                for yh in range(2):
                    plane = pv[pl.ds(n * 128 + yh * 4 + i, 16, stride=8), :]
                    pr[pl.ds(n * 128 + i * 32 + yh * 16, 16), :] = pltpu.roll(plane, by, 1)
        return carry

    lax.fori_loop(0, 8, turn, 0)
    load_cpl.wait()

    for s in range(4):
        for i in range(4):
            cs[pl.ds((s * 4 + i) * 4, 4), :] = cpl_ref[s, i]
    pick = (iota((256, 8), 0) // 32 == iota((256, 8), 1)).astype(F32)
    per_row = lax.dot_general(pick, cs[...], (((1,), (1,)), ((), ())), precision=HI,
                              preferred_element_type=F32)
    r64, c64 = iota((256, 64), 0), iota((256, 64), 1)
    own = ((r64 // 8) % 4 == c64 // 16) & (r64 % 4 == (c64 // 4) % 4)
    per_row = jnp.where(own, per_row, 0.0)
    spread = (iota((64, 256), 0) % 4 == iota((64, 256), 1) % 4).astype(F32)
    wide = lax.dot_general(per_row, spread, (((1,), (0,)), ((), ())), precision=HI,
                           preferred_element_type=F32)
    same = iota((256, 256), 0) // 4 == iota((256, 256), 1) // 4
    mprime[...] = jnp.where(same, wide, 0.0)

    pl.semaphore_wait(barrier, len(others))

    sends = []

    def send(src, dst, k, offset):
        copy = pltpu.make_async_remote_copy(
            src_ref=src, dst_ref=dst, send_sem=hsend.at[k], recv_sem=hrecv.at[k],
            device_id=device(offset), device_id_type=MESH,
        )
        copy.start()
        sends.append(copy)

    send(x_hbm.at[:, :, 8:16, :], ye.at[:, :, 0:8, :], 0, (0, 1, 0))
    send(x_hbm.at[:, :, 0:8, :], ye.at[:, :, 24:32, :], 1, (0, -1, 0))
    send(x_hbm.at[:, 10:16], xe.at[:, 0:6], 2, (1, 0, 0))
    send(x_hbm.at[:, 0:6], xe.at[:, 22:28], 3, (-1, 0, 0))

    load_x.wait()

    flat = xe[:, 6:22].reshape(512, 128)
    fold[...] = flat
    for b in range(2):
        for y in range(16):
            plane = fold[pl.ds(b * 256 + y, 16, stride=16), :]
            xt[b, 16 + y, 16:32, :] = pltpu.roll(plane, 16 * (y % 8), 1) if y % 8 else plane
    row, col = iota((16, 128), 0), iota((16, 128), 1)
    sel = (col == jnp.where(row < 8, 120 + row, row - 8)).astype(F32)
    zs[...] = lax.dot_general(sel, flat, (((1,), (1,)), ((), ())), precision=HI,
                              preferred_element_type=F32)
    send(zs.at[0:8], zr.at[0:8], 4, (0, 0, 1))
    send(zs.at[8:16], zr.at[8:16], 5, (0, 0, -1))
    def gather(n, carry):
        o, s = n >> 2, n & 3
        a, b0, c = place(o, s)
        keep = []
        for y in range(8):
            z = (lane - 16 * (y + b0)) & 127
            keep.append((z >= c) & (z < c + 16))
        acc = [jnp.zeros((8, 128), F32) for _ in range(8)]
        for yh in range(2):
            for h in range(2):
                g = []
                for b in range(2):
                    v = jnp.zeros((8, 128), F32)
                    for y in range(8):
                        w = xt[b, 16 + b0 + 8 * yh + y, pl.ds(16 + a + 8 * h, 8), :]
                        v = jnp.where(keep[y], w, v)
                    g.append(v)
                for i in range(4):
                    p = pr[pl.ds(n * 128 + i * 32 + yh * 16 + h * 8, 8), :]
                    for b in range(2):
                        acc[b * 4 + i] = acc[b * 4 + i] + g[b] * p
        for k in range(8):
            accs[pl.ds(n * 64 + k * 8, 8), :] = acc[k]
        return carry

    lax.fori_loop(0, 32, gather, 0)

    total = accs[pl.ds(0, 256, stride=8), :]
    for k in range(1, 8):
        total = total + accs[pl.ds(k, 256, stride=8), :]
    mine = lax.dot_general(jnp.ones((8, 128), F32), total, (((1,), (1,)), ((), ())),
                           precision=HI, preferred_element_type=F32)
    recv[0] = mine[0:1]
    parts = []
    for k, e in enumerate(others):
        copy = pltpu.make_async_remote_copy(
            src_ref=recv.at[0], dst_ref=recv.at[slot_of(tuple(-v for v in e))],
            send_sem=psend.at[k], recv_sem=precv.at[slot_of(tuple(-v for v in e))],
            device_id=device(e), device_id_type=MESH,
        )
        copy.start()
        parts.append(copy)

    load_y.wait()
    load_pot.wait()
    r128, c128 = iota((128, 128), 0), iota((128, 128), 1)
    near = jnp.where(r128 == c128, -0.5 * 3.0 * COEFF[0], band(r128 - c128))
    base = lax.dot_general(flat, near, (((1,), (0,)), ((), ())), precision=HI,
                           preferred_element_type=F32)
    for copy in sends:
        copy.wait()
    far = band(jnp.where(row < 8, row - 8, 120 + row) - col)
    edge = lax.dot_general(zr[...], far, (((0,), (0,)), ((), ())), precision=HI,
                           preferred_element_type=F32)
    out_ref[...] = base + edge

    def stencil(x, carry):
        for b in range(2):
            here = pl.ds(b * 256 + x * 16, 16)
            acc = pot[x] * xe[b, x + 6] + out_ref[here, :]
            for k in range(1, 7):
                four = (ye[b, x, 8 - k : 24 - k, :] + ye[b, x, 8 + k : 24 + k, :]) + (
                    xe[b, x + 6 - k] + xe[b, x + 6 + k]
                )
                acc = acc + (-0.5 * COEFF[k]) * four
            out_ref[here, :] = acc
        return carry

    lax.fori_loop(0, 16, stencil, 0)

    for copy in parts:
        copy.wait()

    def got(dx, dy, dz):
        r = recv[slot_of((dx, dy, dz))]
        return r[:, 0:128], r[:, 128:256]

    lane1 = iota((1, 128), 1)
    upper_y, upper_z = (lane1 & 64) != 0, (lane1 & 32) != 0
    halves = []
    for h in range(2):
        by_z = {}
        for dz in (-1, 0, 1):
            by_y = {}
            for dy in (-1, 0, 1):
                by_y[dy] = got(0, dy, dz)[h] + got(1 - 2 * h, dy, dz)[1 - h]
            crossed = jnp.where(upper_y, by_y[1], by_y[-1])
            by_z[dz] = by_y[0] + pltpu.roll(crossed, 64, 1)
        down = pltpu.roll(by_z[1], 96, 1)
        up = pltpu.roll(by_z[-1], 32, 1)
        halves.append(by_z[0] + jnp.where(upper_z, up, down))
    sums = jnp.concatenate(halves, axis=1)
    wrep[...] = lax.dot_general(mprime[...] * sums, jnp.ones((256, 128), F32),
                                (((1,), (0,)), ((), ())), precision=HI,
                                preferred_element_type=F32)

    def scatter(o, carry):
        spots = []
        for s in range(4):
            n = o * 4 + s
            live = jnp.where(s < cnt_ref[o], 1.0, 0.0).astype(F32)
            for b in range(2):
                mix = jnp.zeros((32, 128), F32)
                for i in range(4):
                    plane = pr[pl.ds(n * 128 + i * 32, 32), :]
                    mix = mix + plane * (wrep[pl.ds(n * 8 + b * 4 + i, 1), :] * live)
                for yh in range(2):
                    zc[s * 12 + b * 6 + 2 + yh, 16:32, :] = mix[yh * 16 : yh * 16 + 16]
            spots.append(place(o, s))
        for r in range(8):
            keep = []
            z = (lane - 16 * r) & 127
            for a, b0, c in spots:
                keep.append((z >= c) & (z < c + 16))
            for y in (r, r + 8):
                for b in range(2):
                    for h in range(2):
                        acc = sheared[b, y, 8 * h : 8 * h + 8, :]
                        for s, (a, b0, c) in enumerate(spots):
                            w = zc[s * 12 + b * 6 + 2 + ((y - b0) >> 3),
                                   pl.ds(16 - a + 8 * h, 8), :]
                            acc = acc + jnp.where(keep[s], w, 0.0)
                        sheared[b, y, 8 * h : 8 * h + 8, :] = acc
        return carry

    lax.fori_loop(0, 8, scatter, 0)

    for b in range(2):
        for y in range(16):
            plane = sheared[b, y]
            if y % 8:
                plane = pltpu.roll(plane, 128 - 16 * (y % 8), 1)
            out_ref[pl.ds(b * 256 + y, 16, stride=16), :] += plane


def solution(mesh):
    sizes = tuple(mesh.shape[name] for name in ("gx", "gy", "gz"))
    nslots = 1
    for n in sizes:
        nslots *= len(residues(n))

    def on_device(orbitals, potential, projectors, coupling, block_starts, owner_counts):
        rows = projectors.reshape(32, 4, 32, 128).transpose(0, 2, 1, 3).reshape(4096, 128)
        matrices = coupling.reshape(8, 4, 4, 4).transpose(1, 2, 3, 0)
        starts = block_starts.reshape(8, 4, 3).transpose(2, 1, 0)
        counts = owner_counts.reshape(8)
        hbm = pl.BlockSpec(memory_space=pltpu.HBM)
        vmem = pl.BlockSpec(memory_space=pltpu.VMEM)
        return pl.pallas_call(
            functools.partial(kernel, sizes),
            out_shape=jax.ShapeDtypeStruct((512, 128), F32),
            in_specs=[hbm] * 6,
            out_specs=vmem,
            scratch_shapes=[
                pltpu.VMEM((2, 48, 48, 128), F32),
                pltpu.VMEM((2, 28, 16, 128), F32),
                pltpu.VMEM((2, 16, 32, 128), F32),
                pltpu.VMEM((16, 16, 128), F32),
                pltpu.VMEM((4096, 128), F32),
                pltpu.VMEM((4096, 128), F32),
                pltpu.VMEM((2, 16, 16, 128), F32),
                pltpu.VMEM((2048, 128), F32),
                pltpu.VMEM((16, 512), F32),
                pltpu.VMEM((16, 512), F32),
                pltpu.VMEM((nslots, 1, 256), F32),
                pltpu.VMEM((48, 48, 128), F32),
                pltpu.VMEM((256, 128), F32),
                pltpu.VMEM((64, 8), F32),
                pltpu.VMEM((256, 256), F32),
                pltpu.VMEM((512, 128), F32),
                pltpu.VMEM((4, 4, 4, 8), F32),
                pltpu.SMEM((3, 4, 8), jnp.int32),
                pltpu.SMEM((8,), jnp.int32),
                pltpu.SemaphoreType.DMA((7,)),
                pltpu.SemaphoreType.DMA((6,)),
                pltpu.SemaphoreType.DMA((6,)),
                pltpu.SemaphoreType.DMA((nslots,)),
                pltpu.SemaphoreType.DMA((nslots,)),
            ],
            compiler_params=pltpu.CompilerParams(
                collective_id=0, has_side_effects=True, vmem_limit_bytes=60 * 1024 * 1024
            ),
        )(orbitals, potential, rows, matrices, starts, counts).reshape(2, 16, 16, 128)

    in_specs = (
        P(None, "gx", "gy", "gz"),
        P("gx", "gy", "gz"),
        P("gx", "gy", "gz", None, None, None, None),
        P("gx", "gy", "gz", None, None, None, None),
        P("gx", "gy", "gz", None, None, None),
        P("gx", "gy", "gz", None),
    )
    return jax.shard_map(
        on_device, mesh=mesh, in_specs=in_specs,
        out_specs=P(None, "gx", "gy", "gz"), check_vma=False,
    )
```

```python
import functools

import jax
import jax.numpy as jnp
from jax import lax
from jax.experimental import pallas as pl
from jax.experimental.pallas import tpu as pltpu
from jax.sharding import PartitionSpec as P

MESH = pl.DeviceIdType.MESH
HI = lax.Precision.HIGHEST
F32 = jnp.float32
COEFF = [
    -5369.0 / 1800.0,
    12.0 / 7.0,
    -15.0 / 56.0,
    10.0 / 189.0,
    -1.0 / 112.0,
    2.0 / 1925.0,
    -1.0 / 16632.0,
]


def iota(shape, dim):
    return lax.broadcasted_iota(jnp.int32, shape, dim)


def band(distance):
    d = jnp.abs(distance)
    out = jnp.zeros(distance.shape, F32)
    for k in range(1, 7):
        out = jnp.where(d == k, -0.5 * COEFF[k], out)
    return out


def residues(n):
    return [0, 1] if n == 2 else [0, 1, n - 1]


def kernel(
    sizes,
    x_hbm, pot_hbm, p_hbm, cpl_hbm, st_hbm, cnt_hbm,
    out_ref,
    xt, xe, ye, pot, pv, pr, sheared, accs, zs, zr, recv, zc, wrep, cs, mprime, fold,
    cpl_ref, st_ref, cnt_ref,
    lsem, hsend, hrecv, psend, precv,
):
    names = ("gx", "gy", "gz")
    me = [lax.axis_index(name) for name in names]
    res = [residues(n) for n in sizes]
    slots = {}
    for ex in res[0]:
        for ey in res[1]:
            for ez in res[2]:
                slots[(ex, ey, ez)] = len(slots)

    def device(offset):
        return tuple(lax.rem(me[d] + offset[d] % sizes[d], sizes[d]) for d in range(3))

    def slot_of(offset):
        return slots[tuple(offset[d] % sizes[d] for d in range(3))]

    load_x = pltpu.make_async_copy(x_hbm, xe.at[:, 6:22], lsem.at[0])
    load_y = pltpu.make_async_copy(x_hbm, ye.at[:, :, 8:24], lsem.at[1])
    load_p = pltpu.make_async_copy(p_hbm, pv, lsem.at[2])
    load_pot = pltpu.make_async_copy(pot_hbm, pot, lsem.at[3])
    load_st = pltpu.make_async_copy(st_hbm, st_ref, lsem.at[4])
    load_cnt = pltpu.make_async_copy(cnt_hbm, cnt_ref, lsem.at[5])
    load_cpl = pltpu.make_async_copy(cpl_hbm, cpl_ref, lsem.at[6])
    load_st.start()
    load_p.start()
    load_x.start()
    load_cpl.start()
    load_cnt.start()
    load_y.start()
    load_pot.start()

    barrier = pltpu.get_barrier_semaphore()
    others = [e for e in slots if e != (0, 0, 0)]
    for e in others:
        pl.semaphore_signal(barrier, inc=1, device_id=device(e), device_id_type=MESH)

    def clear(i, carry):
        for b in range(2):
            xt[b, i] = jnp.zeros((48, 128), F32)
        return carry

    lax.fori_loop(0, 48, clear, 0)

    def clear_mix(i, carry):
        zc[i] = jnp.zeros((48, 128), F32)
        return carry

    lax.fori_loop(0, 48, clear_mix, 0)

    def clear_sum(i, carry):
        for b in range(2):
            sheared[b, i] = jnp.zeros((16, 128), F32)
        return carry

    lax.fori_loop(0, 16, clear_sum, 0)

    lane = iota((8, 128), 1)

    def place(o, s):
        a = st_ref[0, s, o] - 16 * (o >> 2)
        b0 = st_ref[1, s, o] - 16 * ((o >> 1) & 1)
        c = st_ref[2, s, o] - 128 * (o & 1)
        return a, b0, c

    load_x.wait()

    fold[...] = xe[:, 6:22].reshape(512, 128)
    for b in range(2):
        planes = [fold[pl.ds(b * 256 + y, 16, stride=16), :] for y in range(16)]
        planes = [pltpu.roll(v, 16 * (y % 8), 1) if y % 8 else v for y, v in enumerate(planes)]
        for y, v in enumerate(planes):
            xt[b, 16 + y, 16:32, :] = v

    load_cpl.wait()

    for s in range(4):
        for i in range(4):
            cs[pl.ds((s * 4 + i) * 4, 4), :] = cpl_ref[s, i]
    pick = (iota((256, 8), 0) // 32 == iota((256, 8), 1)).astype(F32)
    per_row = lax.dot_general(pick, cs[...], (((1,), (1,)), ((), ())), precision=HI,
                              preferred_element_type=F32)
    r64, c64 = iota((256, 64), 0), iota((256, 64), 1)
    own = ((r64 // 8) % 4 == c64 // 16) & (r64 % 4 == (c64 // 4) % 4)
    per_row = jnp.where(own, per_row, 0.0)
    spread = (iota((64, 256), 0) % 4 == iota((64, 256), 1) % 4).astype(F32)
    wide = lax.dot_general(per_row, spread, (((1,), (0,)), ((), ())), precision=HI,
                           preferred_element_type=F32)
    same = iota((256, 256), 0) // 4 == iota((256, 256), 1) // 4
    mprime[...] = jnp.where(same, wide, 0.0)

    pl.semaphore_wait(barrier, len(others))

    sends = []

    def send(src, dst, k, offset):
        copy = pltpu.make_async_remote_copy(
            src_ref=src, dst_ref=dst, send_sem=hsend.at[k], recv_sem=hrecv.at[k],
            device_id=device(offset), device_id_type=MESH,
        )
        copy.start()
        sends.append(copy)

    send(x_hbm.at[:, :, 8:16, :], ye.at[:, :, 0:8, :], 0, (0, 1, 0))
    send(x_hbm.at[:, :, 0:8, :], ye.at[:, :, 24:32, :], 1, (0, -1, 0))
    send(x_hbm.at[:, 10:16], xe.at[:, 0:6], 2, (1, 0, 0))
    send(x_hbm.at[:, 0:6], xe.at[:, 22:28], 3, (-1, 0, 0))

    load_st.wait()
    load_cnt.wait()
    load_p.wait()

    def turn(o, carry):
        for s in range(4):
            n = o * 4 + s
            _, b0, c = place(o, s)
            by = (c + 16 * b0) & 127
            planes = [
                pltpu.roll(pv[pl.ds(n * 128 + yh * 4 + i, 16, stride=8), :], by, 1)
                for i in range(4) for yh in range(2)
            ]
            for k, plane in enumerate(planes):
                pr[pl.ds(n * 128 + k * 16, 16), :] = plane
        return carry

    lax.fori_loop(0, 8, turn, 0)
    def gather(n, carry):
        o, s = n >> 2, n & 3
        a, b0, c = place(o, s)
        keep = []
        for y in range(8):
            z = (lane - 16 * (y + b0)) & 127
            keep.append((z >= c) & (z < c + 16))
        acc = [jnp.zeros((8, 128), F32) for _ in range(8)]
        for yh in range(2):
            for h in range(2):
                g = []
                for b in range(2):
                    v = jnp.zeros((8, 128), F32)
                    for y in range(8):
                        w = xt[b, 16 + b0 + 8 * yh + y, pl.ds(16 + a + 8 * h, 8), :]
                        v = jnp.where(keep[y], w, v)
                    g.append(v)
                for i in range(4):
                    p = pr[pl.ds(n * 128 + i * 32 + yh * 16 + h * 8, 8), :]
                    for b in range(2):
                        acc[b * 4 + i] = acc[b * 4 + i] + g[b] * p
        for k in range(8):
            accs[pl.ds(n * 64 + k * 8, 8), :] = acc[k]
        return carry

    lax.fori_loop(0, 32, gather, 0)

    total = accs[pl.ds(0, 256, stride=8), :]
    for k in range(1, 8):
        total = total + accs[pl.ds(k, 256, stride=8), :]
    mine = lax.dot_general(jnp.ones((8, 128), F32), total, (((1,), (1,)), ((), ())),
                           precision=HI, preferred_element_type=F32)
    recv[0] = mine[0:1]
    parts = []
    for k, e in enumerate(others):
        copy = pltpu.make_async_remote_copy(
            src_ref=recv.at[0], dst_ref=recv.at[slot_of(tuple(-v for v in e))],
            send_sem=psend.at[k], recv_sem=precv.at[slot_of(tuple(-v for v in e))],
            device_id=device(e), device_id_type=MESH,
        )
        copy.start()
        parts.append(copy)

    row, col = iota((16, 128), 0), iota((16, 128), 1)
    sel = (col == jnp.where(row < 8, 120 + row, row - 8)).astype(F32)
    zs[...] = lax.dot_general(sel, fold[...], (((1,), (1,)), ((), ())), precision=HI,
                              preferred_element_type=F32)
    send(zs.at[0:8], zr.at[0:8], 4, (0, 0, 1))
    send(zs.at[8:16], zr.at[8:16], 5, (0, 0, -1))
    load_y.wait()
    load_pot.wait()
    r128, c128 = iota((128, 128), 0), iota((128, 128), 1)
    near = jnp.where(r128 == c128, -0.5 * 3.0 * COEFF[0], band(r128 - c128))
    base = lax.dot_general(fold[...], near, (((1,), (0,)), ((), ())), precision=HI,
                           preferred_element_type=F32)
    for copy in sends:
        copy.wait()
    far = band(jnp.where(row < 8, row - 8, 120 + row) - col)
    edge = lax.dot_general(zr[...], far, (((0,), (0,)), ((), ())), precision=HI,
                           preferred_element_type=F32)
    out_ref[...] = base + edge

    def stencil(x, carry):
        done = []
        for b in range(2):
            here = pl.ds(b * 256 + x * 16, 16)
            acc = pot[x] * xe[b, x + 6] + out_ref[here, :]
            for k in range(1, 7):
                four = (ye[b, x, 8 - k : 24 - k, :] + ye[b, x, 8 + k : 24 + k, :]) + (
                    xe[b, x + 6 - k] + xe[b, x + 6 + k]
                )
                acc = acc + (-0.5 * COEFF[k]) * four
            done.append(acc)
        for b in range(2):
            out_ref[pl.ds(b * 256 + x * 16, 16), :] = done[b]
        return carry

    lax.fori_loop(0, 16, stencil, 0)

    for copy in parts:
        copy.wait()

    def got(dx, dy, dz):
        r = recv[slot_of((dx, dy, dz))]
        return r[:, 0:128], r[:, 128:256]

    lane1 = iota((1, 128), 1)
    upper_y, upper_z = (lane1 & 64) != 0, (lane1 & 32) != 0
    halves = []
    for h in range(2):
        by_z = {}
        for dz in (-1, 0, 1):
            by_y = {}
            for dy in (-1, 0, 1):
                by_y[dy] = got(0, dy, dz)[h] + got(1 - 2 * h, dy, dz)[1 - h]
            crossed = jnp.where(upper_y, by_y[1], by_y[-1])
            by_z[dz] = by_y[0] + pltpu.roll(crossed, 64, 1)
        down = pltpu.roll(by_z[1], 96, 1)
        up = pltpu.roll(by_z[-1], 32, 1)
        halves.append(by_z[0] + jnp.where(upper_z, up, down))
    sums = jnp.concatenate(halves, axis=1)
    wrep[...] = lax.dot_general(mprime[...] * sums, jnp.ones((256, 128), F32),
                                (((1,), (0,)), ((), ())), precision=HI,
                                preferred_element_type=F32)

    def scatter(o, carry):
        spots, mixes = [], []
        for s in range(4):
            n = o * 4 + s
            live = jnp.where(s < cnt_ref[o], 1.0, 0.0).astype(F32)
            for b in range(2):
                mix = jnp.zeros((32, 128), F32)
                for i in range(4):
                    plane = pr[pl.ds(n * 128 + i * 32, 32), :]
                    mix = mix + plane * (wrep[pl.ds(n * 8 + b * 4 + i, 1), :] * live)
                mixes.append(mix)
            spots.append(place(o, s))
        for k, mix in enumerate(mixes):
            for yh in range(2):
                zc[k * 6 + 2 + yh, 16:32, :] = mix[yh * 16 : yh * 16 + 16]
        for r in range(8):
            keep = []
            z = (lane - 16 * r) & 127
            for a, b0, c in spots:
                keep.append((z >= c) & (z < c + 16))
            where = [(b, y, h) for y in (r, r + 8) for b in range(2) for h in range(2)]
            sums = []
            for b, y, h in where:
                acc = sheared[b, y, 8 * h : 8 * h + 8, :]
                for s, (a, b0, c) in enumerate(spots):
                    w = zc[s * 12 + b * 6 + 2 + ((y - b0) >> 3), pl.ds(16 - a + 8 * h, 8), :]
                    acc = acc + jnp.where(keep[s], w, 0.0)
                sums.append(acc)
            for (b, y, h), acc in zip(where, sums):
                sheared[b, y, 8 * h : 8 * h + 8, :] = acc
        return carry

    lax.fori_loop(0, 8, scatter, 0)

    for b in range(2):
        planes = [sheared[b, y] for y in range(16)]
        planes = [
            (pltpu.roll(v, 128 - 16 * (y % 8), 1) if y % 8 else v)
            + out_ref[pl.ds(b * 256 + y, 16, stride=16), :]
            for y, v in enumerate(planes)
        ]
        for y, v in enumerate(planes):
            out_ref[pl.ds(b * 256 + y, 16, stride=16), :] = v


def solution(mesh):
    sizes = tuple(mesh.shape[name] for name in ("gx", "gy", "gz"))
    nslots = 1
    for n in sizes:
        nslots *= len(residues(n))

    def on_device(orbitals, potential, projectors, coupling, block_starts, owner_counts):
        rows = projectors.reshape(32, 4, 32, 128).transpose(0, 2, 1, 3).reshape(4096, 128)
        matrices = coupling.reshape(8, 4, 4, 4).transpose(1, 2, 3, 0)
        starts = block_starts.reshape(8, 4, 3).transpose(2, 1, 0)
        counts = owner_counts.reshape(8)
        hbm = pl.BlockSpec(memory_space=pltpu.HBM)
        vmem = pl.BlockSpec(memory_space=pltpu.VMEM)
        return pl.pallas_call(
            functools.partial(kernel, sizes),
            out_shape=jax.ShapeDtypeStruct((512, 128), F32),
            in_specs=[hbm] * 6,
            out_specs=vmem,
            scratch_shapes=[
                pltpu.VMEM((2, 48, 48, 128), F32),
                pltpu.VMEM((2, 28, 16, 128), F32),
                pltpu.VMEM((2, 16, 32, 128), F32),
                pltpu.VMEM((16, 16, 128), F32),
                pltpu.VMEM((4096, 128), F32),
                pltpu.VMEM((4096, 128), F32),
                pltpu.VMEM((2, 16, 16, 128), F32),
                pltpu.VMEM((2048, 128), F32),
                pltpu.VMEM((16, 512), F32),
                pltpu.VMEM((16, 512), F32),
                pltpu.VMEM((nslots, 1, 256), F32),
                pltpu.VMEM((48, 48, 128), F32),
                pltpu.VMEM((256, 128), F32),
                pltpu.VMEM((64, 8), F32),
                pltpu.VMEM((256, 256), F32),
                pltpu.VMEM((512, 128), F32),
                pltpu.VMEM((4, 4, 4, 8), F32),
                pltpu.SMEM((3, 4, 8), jnp.int32),
                pltpu.SMEM((8,), jnp.int32),
                pltpu.SemaphoreType.DMA((7,)),
                pltpu.SemaphoreType.DMA((6,)),
                pltpu.SemaphoreType.DMA((6,)),
                pltpu.SemaphoreType.DMA((nslots,)),
                pltpu.SemaphoreType.DMA((nslots,)),
            ],
            compiler_params=pltpu.CompilerParams(
                collective_id=0, has_side_effects=True, vmem_limit_bytes=60 * 1024 * 1024
            ),
        )(orbitals, potential, rows, matrices, starts, counts).reshape(2, 16, 16, 128)

    in_specs = (
        P(None, "gx", "gy", "gz"),
        P("gx", "gy", "gz"),
        P("gx", "gy", "gz", None, None, None, None),
        P("gx", "gy", "gz", None, None, None, None),
        P("gx", "gy", "gz", None, None, None),
        P("gx", "gy", "gz", None),
    )
    return jax.shard_map(
        on_device, mesh=mesh, in_specs=in_specs,
        out_specs=P(None, "gx", "gy", "gz"), check_vma=False,
    )
```

```python
import functools

import jax
import jax.numpy as jnp
from jax import lax
from jax.experimental import pallas as pl
from jax.experimental.pallas import tpu as pltpu
from jax.sharding import PartitionSpec as P

MESH = pl.DeviceIdType.MESH
HI = lax.Precision.HIGHEST
F32 = jnp.float32
COEFF = [
    -5369.0 / 1800.0,
    12.0 / 7.0,
    -15.0 / 56.0,
    10.0 / 189.0,
    -1.0 / 112.0,
    2.0 / 1925.0,
    -1.0 / 16632.0,
]


def iota(shape, dim):
    return lax.broadcasted_iota(jnp.int32, shape, dim)


def band(distance):
    d = jnp.abs(distance)
    out = jnp.zeros(distance.shape, F32)
    for k in range(1, 7):
        out = jnp.where(d == k, -0.5 * COEFF[k], out)
    return out


def residues(n):
    return [0, 1] if n == 2 else [0, 1, n - 1]


def kernel(
    sizes,
    x_hbm, pot_hbm, p_hbm, cpl_hbm, st_hbm, cnt_hbm,
    out_ref,
    xt, xe, ye, pot, pv, pr, sheared, accs, zs, zr, recv, zc, wrep, cs, mprime, fold,
    cpl_ref, st_ref, cnt_ref,
    lsem, hsend, hrecv, psend, precv,
):
    names = ("gx", "gy", "gz")
    me = [lax.axis_index(name) for name in names]
    res = [residues(n) for n in sizes]
    slots = {}
    for ex in res[0]:
        for ey in res[1]:
            for ez in res[2]:
                slots[(ex, ey, ez)] = len(slots)

    def device(offset):
        return tuple(lax.rem(me[d] + offset[d] % sizes[d], sizes[d]) for d in range(3))

    def slot_of(offset):
        return slots[tuple(offset[d] % sizes[d] for d in range(3))]

    load_x = pltpu.make_async_copy(x_hbm, xe.at[:, 6:22], lsem.at[0])
    load_y = pltpu.make_async_copy(x_hbm, ye.at[:, :, 8:24], lsem.at[1])
    load_p = [
        pltpu.make_async_copy(p_hbm.at[pl.ds(k * 1024, 1024)], pv.at[pl.ds(k * 1024, 1024)],
                              lsem.at[7 + k])
        for k in range(4)
    ]
    load_pot = pltpu.make_async_copy(pot_hbm, pot, lsem.at[3])
    load_st = pltpu.make_async_copy(st_hbm, st_ref, lsem.at[4])
    load_cnt = pltpu.make_async_copy(cnt_hbm, cnt_ref, lsem.at[5])
    load_cpl = pltpu.make_async_copy(cpl_hbm, cpl_ref, lsem.at[6])
    load_st.start()
    for copy in load_p:
        copy.start()
    load_x.start()
    load_cpl.start()
    load_cnt.start()
    load_y.start()
    load_pot.start()

    barrier = pltpu.get_barrier_semaphore()
    others = [e for e in slots if e != (0, 0, 0)]
    for e in others:
        pl.semaphore_signal(barrier, inc=1, device_id=device(e), device_id_type=MESH)

    def clear(i, carry):
        xt[pl.ds(i * 96, 96), :] = jnp.zeros((96, 128), F32)
        return carry

    lax.fori_loop(0, 48, clear, 0)

    def clear_mix(i, carry):
        zc[pl.ds(i * 96, 96), :] = jnp.zeros((96, 128), F32)
        return carry

    lax.fori_loop(0, 24, clear_mix, 0)

    def clear_sum(i, carry):
        for b in range(2):
            sheared[b, i] = jnp.zeros((16, 128), F32)
        return carry

    lax.fori_loop(0, 16, clear_sum, 0)

    lane = iota((8, 128), 1)

    def place(o, s):
        a = st_ref[0, s, o] - 16 * (o >> 2)
        b0 = st_ref[1, s, o] - 16 * ((o >> 1) & 1)
        c = st_ref[2, s, o] - 128 * (o & 1)
        return a, b0, c

    load_x.wait()

    fold[...] = xe[:, 6:22].reshape(512, 128)
    for b in range(2):
        planes = [fold[pl.ds(b * 256 + y, 16, stride=16), :] for y in range(16)]
        planes = [pltpu.roll(v, 16 * (y % 8), 1) if y % 8 else v for y, v in enumerate(planes)]
        for y, v in enumerate(planes):
            xt[b * 2304 + (16 + y) * 48 + 16 : b * 2304 + (16 + y) * 48 + 32, :] = v

    pl.semaphore_wait(barrier, len(others))

    sends = []

    def send(src, dst, k, offset):
        copy = pltpu.make_async_remote_copy(
            src_ref=src, dst_ref=dst, send_sem=hsend.at[k], recv_sem=hrecv.at[k],
            device_id=device(offset), device_id_type=MESH,
        )
        copy.start()
        sends.append(copy)

    send(x_hbm.at[:, :, 8:16, :], ye.at[:, :, 0:8, :], 0, (0, 1, 0))
    send(x_hbm.at[:, :, 0:8, :], ye.at[:, :, 24:32, :], 1, (0, -1, 0))
    send(x_hbm.at[:, 10:16], xe.at[:, 0:6], 2, (1, 0, 0))
    send(x_hbm.at[:, 0:6], xe.at[:, 22:28], 3, (-1, 0, 0))

    load_st.wait()
    load_cnt.wait()

    def turn(o, carry):
        for s in range(4):
            n = o * 4 + s
            _, b0, c = place(o, s)
            by = (c + 16 * b0) & 127
            planes = [
                pltpu.roll(pv[pl.ds(n * 128 + yh * 4 + i, 16, stride=8), :], by, 1)
                for i in range(4) for yh in range(2)
            ]
            for k, plane in enumerate(planes):
                pr[pl.ds(n * 128 + k * 16, 16), :] = plane
        return carry

    for k in range(4):
        load_p[k].wait()
        lax.fori_loop(2 * k, 2 * k + 2, turn, 0)

    def gather(n, carry):
        o, s = n >> 2, n & 3
        a, b0, c = place(o, s)
        corner = (16 + b0) * 48 + 16 + a
        keep = []
        for y in range(8):
            z = (lane - 16 * (y + b0)) & 127
            keep.append((z >= c) & (z < c + 16))
        acc = [jnp.zeros((8, 128), F32) for _ in range(8)]
        for yh in range(2):
            for h in range(2):
                g = []
                for b in range(2):
                    v = jnp.zeros((8, 128), F32)
                    for y in range(8):
                        w = xt[pl.ds(corner + (b * 2304 + (8 * yh + y) * 48 + 8 * h), 8), :]
                        v = jnp.where(keep[y], w, v)
                    g.append(v)
                for i in range(4):
                    p = pr[pl.ds(n * 128 + i * 32 + yh * 16 + h * 8, 8), :]
                    for b in range(2):
                        acc[b * 4 + i] = acc[b * 4 + i] + g[b] * p
        for k in range(8):
            accs[pl.ds(n * 64 + k * 8, 8), :] = acc[k]
        return carry

    lax.fori_loop(0, 32, gather, 0)

    total = accs[pl.ds(0, 256, stride=8), :]
    for k in range(1, 8):
        total = total + accs[pl.ds(k, 256, stride=8), :]
    mine = lax.dot_general(jnp.ones((8, 128), F32), total, (((1,), (1,)), ((), ())),
                           precision=HI, preferred_element_type=F32)
    recv[0] = mine[0:1]
    parts = []
    for k, e in enumerate(others):
        copy = pltpu.make_async_remote_copy(
            src_ref=recv.at[0], dst_ref=recv.at[slot_of(tuple(-v for v in e))],
            send_sem=psend.at[k], recv_sem=precv.at[slot_of(tuple(-v for v in e))],
            device_id=device(e), device_id_type=MESH,
        )
        copy.start()
        parts.append(copy)

    row, col = iota((16, 128), 0), iota((16, 128), 1)
    sel = (col == jnp.where(row < 8, 120 + row, row - 8)).astype(F32)
    zs[...] = lax.dot_general(sel, fold[...], (((1,), (1,)), ((), ())), precision=HI,
                              preferred_element_type=F32)
    send(zs.at[0:8], zr.at[0:8], 4, (0, 0, 1))
    send(zs.at[8:16], zr.at[8:16], 5, (0, 0, -1))
    load_y.wait()
    load_pot.wait()
    r128, c128 = iota((128, 128), 0), iota((128, 128), 1)
    near = jnp.where(r128 == c128, -0.5 * 3.0 * COEFF[0], band(r128 - c128))
    out_ref[...] = lax.dot_general(fold[...], near, (((1,), (0,)), ((), ())), precision=HI,
                           preferred_element_type=F32)
    for copy in sends[:4]:
        copy.wait()

    def stencil(x, carry):
        done = []
        for b in range(2):
            here = pl.ds(b * 256 + x * 16, 16)
            acc = pot[x] * xe[b, x + 6] + out_ref[here, :]
            for k in range(1, 7):
                four = (ye[b, x, 8 - k : 24 - k, :] + ye[b, x, 8 + k : 24 + k, :]) + (
                    xe[b, x + 6 - k] + xe[b, x + 6 + k]
                )
                acc = acc + (-0.5 * COEFF[k]) * four
            done.append(acc)
        for b in range(2):
            out_ref[pl.ds(b * 256 + x * 16, 16), :] = done[b]
        return carry

    lax.fori_loop(0, 16, stencil, 0)

    load_cpl.wait()

    for s in range(4):
        for i in range(4):
            cs[pl.ds((s * 4 + i) * 4, 4), :] = cpl_ref[s, i]
    pick = (iota((256, 8), 0) // 32 == iota((256, 8), 1)).astype(F32)
    per_row = lax.dot_general(pick, cs[...], (((1,), (1,)), ((), ())), precision=HI,
                              preferred_element_type=F32)
    r64, c64 = iota((256, 64), 0), iota((256, 64), 1)
    own = ((r64 // 8) % 4 == c64 // 16) & (r64 % 4 == (c64 // 4) % 4)
    per_row = jnp.where(own, per_row, 0.0)
    spread = (iota((64, 256), 0) % 4 == iota((64, 256), 1) % 4).astype(F32)
    wide = lax.dot_general(per_row, spread, (((1,), (0,)), ((), ())), precision=HI,
                           preferred_element_type=F32)
    same = iota((256, 256), 0) // 4 == iota((256, 256), 1) // 4
    mprime[...] = jnp.where(same, wide, 0.0)

    for copy in sends[4:]:
        copy.wait()
    far = band(jnp.where(row < 8, row - 8, 120 + row) - col)
    edge = lax.dot_general(zr[...], far, (((0,), (0,)), ((), ())), precision=HI,
                           preferred_element_type=F32)
    out_ref[...] += edge


    for copy in parts:
        copy.wait()

    def got(dx, dy, dz):
        r = recv[slot_of((dx, dy, dz))]
        return r[:, 0:128], r[:, 128:256]

    lane1 = iota((1, 128), 1)
    upper_y, upper_z = (lane1 & 64) != 0, (lane1 & 32) != 0
    halves = []
    for h in range(2):
        by_z = {}
        for dz in (-1, 0, 1):
            by_y = {}
            for dy in (-1, 0, 1):
                by_y[dy] = got(0, dy, dz)[h] + got(1 - 2 * h, dy, dz)[1 - h]
            crossed = jnp.where(upper_y, by_y[1], by_y[-1])
            by_z[dz] = by_y[0] + pltpu.roll(crossed, 64, 1)
        down = pltpu.roll(by_z[1], 96, 1)
        up = pltpu.roll(by_z[-1], 32, 1)
        halves.append(by_z[0] + jnp.where(upper_z, up, down))
    sums = jnp.concatenate(halves, axis=1)
    wrep[...] = lax.dot_general(mprime[...] * sums, jnp.ones((256, 128), F32),
                                (((1,), (0,)), ((), ())), precision=HI,
                                preferred_element_type=F32)

    def scatter(o, carry):
        spots, mixes = [], []
        for s in range(4):
            n = o * 4 + s
            live = jnp.where(s < cnt_ref[o], 1.0, 0.0).astype(F32)
            for b in range(2):
                mix = jnp.zeros((32, 128), F32)
                for i in range(4):
                    plane = pr[pl.ds(n * 128 + i * 32, 32), :]
                    mix = mix + plane * (wrep[pl.ds(n * 8 + b * 4 + i, 1), :] * live)
                mixes.append(mix)
            spots.append(place(o, s))
        for k, mix in enumerate(mixes):
            for yh in range(2):
                zc[(k * 6 + 2 + yh) * 48 + 16 : (k * 6 + 2 + yh) * 48 + 32, :] = mix[yh * 16 : yh * 16 + 16]
        for r in range(8):
            keep = []
            z = (lane - 16 * r) & 127
            for a, b0, c in spots:
                keep.append((z >= c) & (z < c + 16))
            corner = {
                (s, y): ((y - b0) >> 3) * 48 - a
                for s, (a, b0, c) in enumerate(spots) for y in (r, r + 8)
            }
            where = [(b, y, h) for y in (r, r + 8) for b in range(2) for h in range(2)]
            sums = []
            for b, y, h in where:
                acc = sheared[b, y, 8 * h : 8 * h + 8, :]
                for s in range(4):
                    at = (s * 12 + b * 6 + 2) * 48 + 16 + 8 * h
                    w = zc[pl.ds(corner[s, y] + at, 8), :]
                    acc = acc + jnp.where(keep[s], w, 0.0)
                sums.append(acc)
            for (b, y, h), acc in zip(where, sums):
                sheared[b, y, 8 * h : 8 * h + 8, :] = acc
        return carry

    lax.fori_loop(0, 8, scatter, 0)

    for b in range(2):
        planes = [sheared[b, y] for y in range(16)]
        planes = [
            (pltpu.roll(v, 128 - 16 * (y % 8), 1) if y % 8 else v)
            + out_ref[pl.ds(b * 256 + y, 16, stride=16), :]
            for y, v in enumerate(planes)
        ]
        for y, v in enumerate(planes):
            out_ref[pl.ds(b * 256 + y, 16, stride=16), :] = v


def solution(mesh):
    sizes = tuple(mesh.shape[name] for name in ("gx", "gy", "gz"))
    nslots = 1
    for n in sizes:
        nslots *= len(residues(n))

    def on_device(orbitals, potential, projectors, coupling, block_starts, owner_counts):
        rows = projectors.reshape(32, 4, 32, 128).transpose(0, 2, 1, 3).reshape(4096, 128)
        matrices = coupling.reshape(8, 4, 4, 4).transpose(1, 2, 3, 0)
        starts = block_starts.reshape(8, 4, 3).transpose(2, 1, 0)
        counts = owner_counts.reshape(8)
        hbm = pl.BlockSpec(memory_space=pltpu.HBM)
        vmem = pl.BlockSpec(memory_space=pltpu.VMEM)
        return pl.pallas_call(
            functools.partial(kernel, sizes),
            out_shape=jax.ShapeDtypeStruct((512, 128), F32),
            in_specs=[hbm] * 6,
            out_specs=vmem,
            scratch_shapes=[
                pltpu.VMEM((4608, 128), F32),
                pltpu.VMEM((2, 28, 16, 128), F32),
                pltpu.VMEM((2, 16, 32, 128), F32),
                pltpu.VMEM((16, 16, 128), F32),
                pltpu.VMEM((4096, 128), F32),
                pltpu.VMEM((4096, 128), F32),
                pltpu.VMEM((2, 16, 16, 128), F32),
                pltpu.VMEM((2048, 128), F32),
                pltpu.VMEM((16, 512), F32),
                pltpu.VMEM((16, 512), F32),
                pltpu.VMEM((nslots, 1, 256), F32),
                pltpu.VMEM((2304, 128), F32),
                pltpu.VMEM((256, 128), F32),
                pltpu.VMEM((64, 8), F32),
                pltpu.VMEM((256, 256), F32),
                pltpu.VMEM((512, 128), F32),
                pltpu.VMEM((4, 4, 4, 8), F32),
                pltpu.SMEM((3, 4, 8), jnp.int32),
                pltpu.SMEM((8,), jnp.int32),
                pltpu.SemaphoreType.DMA((11,)),
                pltpu.SemaphoreType.DMA((6,)),
                pltpu.SemaphoreType.DMA((6,)),
                pltpu.SemaphoreType.DMA((nslots,)),
                pltpu.SemaphoreType.DMA((nslots,)),
            ],
            compiler_params=pltpu.CompilerParams(
                collective_id=0, has_side_effects=True, vmem_limit_bytes=60 * 1024 * 1024
            ),
        )(orbitals, potential, rows, matrices, starts, counts).reshape(2, 16, 16, 128)

    in_specs = (
        P(None, "gx", "gy", "gz"),
        P("gx", "gy", "gz"),
        P("gx", "gy", "gz", None, None, None, None),
        P("gx", "gy", "gz", None, None, None, None),
        P("gx", "gy", "gz", None, None, None),
        P("gx", "gy", "gz", None),
    )
    return jax.shard_map(
        on_device, mesh=mesh, in_specs=in_specs,
        out_specs=P(None, "gx", "gy", "gz"), check_vma=False,
    )
```

```python
import functools

import jax
import jax.numpy as jnp
from jax import lax
from jax.experimental import pallas as pl
from jax.experimental.pallas import tpu as pltpu
from jax.sharding import PartitionSpec as P

MESH = pl.DeviceIdType.MESH
HI = lax.Precision.HIGHEST
F32 = jnp.float32
COEFF = [
    -5369.0 / 1800.0,
    12.0 / 7.0,
    -15.0 / 56.0,
    10.0 / 189.0,
    -1.0 / 112.0,
    2.0 / 1925.0,
    -1.0 / 16632.0,
]


def iota(shape, dim):
    return lax.broadcasted_iota(jnp.int32, shape, dim)


def band(distance):
    d = jnp.abs(distance)
    out = jnp.zeros(distance.shape, F32)
    for k in range(1, 7):
        out = jnp.where(d == k, -0.5 * COEFF[k], out)
    return out


def split3(v):
    hi = v.astype(jnp.bfloat16)
    left = v - hi.astype(F32)
    mid = left.astype(jnp.bfloat16)
    low = (left - mid.astype(F32)).astype(jnp.bfloat16)
    return hi, mid, low


def exact_dot(v, units, dims, flip=False):
    units = units.astype(jnp.bfloat16)
    total = None
    for term in reversed(split3(v)):
        pair = (units, term) if flip else (term, units)
        out = lax.dot_general(*pair, (dims, ((), ())), preferred_element_type=F32)
        total = out if total is None else total + out
    return total


def residues(n):
    return [0, 1] if n == 2 else [0, 1, n - 1]


def kernel(
    sizes,
    x_hbm, pot_hbm, p_hbm, cpl_hbm, st_hbm, cnt_hbm,
    out_hbm,
    base, xt, xe, ye, pot, pv, pr, sheared, accs, zs, zr, recv, zc, wrep, cs, mprime, fold,
    cpl_ref, st_ref, cnt_ref,
    lsem, hsend, hrecv, psend, precv,
):
    names = ("gx", "gy", "gz")
    me = [lax.axis_index(name) for name in names]
    res = [residues(n) for n in sizes]
    slots = {}
    for ex in res[0]:
        for ey in res[1]:
            for ez in res[2]:
                slots[(ex, ey, ez)] = len(slots)

    def device(offset):
        return tuple(lax.rem(me[d] + offset[d] % sizes[d], sizes[d]) for d in range(3))

    def slot_of(offset):
        return slots[tuple(offset[d] % sizes[d] for d in range(3))]

    load_x = pltpu.make_async_copy(x_hbm, xe.at[:, 6:22], lsem.at[0])
    load_y = pltpu.make_async_copy(x_hbm, ye.at[:, :, 8:24], lsem.at[1])
    load_p = [
        pltpu.make_async_copy(p_hbm.at[pl.ds(k * 1024, 1024)], pv.at[pl.ds(k * 1024, 1024)],
                              lsem.at[7 + k])
        for k in range(4)
    ]
    load_pot = pltpu.make_async_copy(pot_hbm, pot, lsem.at[3])
    load_st = pltpu.make_async_copy(st_hbm, st_ref, lsem.at[4])
    load_cnt = pltpu.make_async_copy(cnt_hbm, cnt_ref, lsem.at[5])
    load_cpl = pltpu.make_async_copy(cpl_hbm, cpl_ref, lsem.at[6])
    load_st.start()
    for copy in load_p:
        copy.start()
    load_x.start()
    load_cpl.start()
    load_cnt.start()
    load_y.start()
    load_pot.start()

    barrier = pltpu.get_barrier_semaphore()
    others = [e for e in slots if e != (0, 0, 0)]
    others.sort(key=lambda e: -sum(e))
    for e in others:
        pl.semaphore_signal(barrier, inc=1, device_id=device(e), device_id_type=MESH)

    def clear(i, carry):
        xt[pl.ds(i * 96, 96), :] = jnp.zeros((96, 128), F32)
        return carry

    lax.fori_loop(0, 48, clear, 0)

    def clear_mix(i, carry):
        zc[pl.ds(i * 96, 96), :] = jnp.zeros((96, 128), F32)
        return carry

    lax.fori_loop(0, 24, clear_mix, 0)

    def clear_sum(i, carry):
        for b in range(2):
            sheared[b, i] = jnp.zeros((16, 128), F32)
        return carry

    lax.fori_loop(0, 16, clear_sum, 0)

    lane = iota((8, 128), 1)

    def place(o, s):
        a = st_ref[0, s, o] - 16 * (o >> 2)
        b0 = st_ref[1, s, o] - 16 * ((o >> 1) & 1)
        c = st_ref[2, s, o] - 128 * (o & 1)
        return a, b0, c

    load_x.wait()

    fold[...] = xe[:, 6:22].reshape(512, 128)
    for b in range(2):
        planes = [fold[pl.ds(b * 256 + y, 16, stride=16), :] for y in range(16)]
        planes = [pltpu.roll(v, 16 * (y % 8), 1) if y % 8 else v for y, v in enumerate(planes)]
        for y, v in enumerate(planes):
            xt[b * 2304 + (16 + y) * 48 + 16 : b * 2304 + (16 + y) * 48 + 32, :] = v

    row, col = iota((16, 128), 0), iota((16, 128), 1)
    sel = (col == jnp.where(row < 8, 120 + row, row - 8)).astype(F32)
    zs[...] = exact_dot(fold[...], sel, ((1,), (1,)), flip=True)
    pl.semaphore_wait(barrier, len(others))

    sends = []

    def send(src, dst, k, offset):
        copy = pltpu.make_async_remote_copy(
            src_ref=src, dst_ref=dst, send_sem=hsend.at[k], recv_sem=hrecv.at[k],
            device_id=device(offset), device_id_type=MESH,
        )
        copy.start()
        sends.append(copy)

    send(x_hbm.at[:, :, 8:16, :], ye.at[:, :, 0:8, :], 0, (0, 1, 0))
    send(x_hbm.at[:, :, 0:8, :], ye.at[:, :, 24:32, :], 1, (0, -1, 0))
    send(x_hbm.at[:, 10:16], xe.at[:, 0:6], 2, (1, 0, 0))
    send(x_hbm.at[:, 0:6], xe.at[:, 22:28], 3, (-1, 0, 0))
    send(zs.at[0:8], zr.at[0:8], 4, (0, 0, 1))
    send(zs.at[8:16], zr.at[8:16], 5, (0, 0, -1))

    load_st.wait()
    load_cnt.wait()

    def gather(pair, carry):
        kept = []
        for u in range(2):
            n = pair * 2 + u
            a, b0, c = place(n >> 2, n & 3)
            by = (c + 16 * b0) & 127
            planes = [
                pltpu.roll(pv[pl.ds(n * 128 + yh * 4 + i, 16, stride=8), :], by, 1)
                for i in range(4) for yh in range(2)
            ]
            corner = (16 + b0) * 48 + 16 + a
            keep = []
            for y in range(8):
                z = (lane - 16 * (y + b0)) & 127
                keep.append((z >= c) & (z < c + 16))
            acc = [None] * 8
            for yh in range(2):
                for h in range(2):
                    g = []
                    for b in range(2):
                        v = jnp.zeros((8, 128), F32)
                        for y in range(8):
                            at = b * 2304 + (8 * yh + y) * 48 + 8 * h
                            v = jnp.where(keep[y], xt[pl.ds(corner + at, 8), :], v)
                        g.append(v)
                    for i in range(4):
                        p = planes[i * 2 + yh][8 * h : 8 * h + 8]
                        for b in range(2):
                            term = g[b] * p
                            k = b * 4 + i
                            acc[k] = term if acc[k] is None else acc[k] + term
            kept.append((n, planes, acc))
        for n, planes, acc in kept:
            for k, plane in enumerate(planes):
                pr[pl.ds(n * 128 + k * 16, 16), :] = plane
            for k in range(8):
                accs[pl.ds(n * 64 + k * 8, 8), :] = acc[k]
        return carry

    for k in range(4):
        load_p[k].wait()
        lax.fori_loop(4 * k, 4 * k + 4, gather, 0)

    total = accs[pl.ds(0, 256, stride=8), :]
    for k in range(1, 8):
        total = total + accs[pl.ds(k, 256, stride=8), :]
    mine = exact_dot(total, jnp.ones((8, 128), F32), ((1,), (1,)), flip=True)
    recv[0] = mine[0:1]
    parts = []
    for k, e in enumerate(others):
        copy = pltpu.make_async_remote_copy(
            src_ref=recv.at[0], dst_ref=recv.at[slot_of(tuple(-v for v in e))],
            send_sem=psend.at[k], recv_sem=precv.at[slot_of(tuple(-v for v in e))],
            device_id=device(e), device_id_type=MESH,
        )
        copy.start()
        parts.append(copy)

    load_y.wait()
    load_pot.wait()
    r128, c128 = iota((128, 128), 0), iota((128, 128), 1)
    near = jnp.where(r128 == c128, -0.5 * 3.0 * COEFF[0], band(r128 - c128))
    base[...] = lax.dot_general(fold[...], near, (((1,), (0,)), ((), ())), precision=HI,
                           preferred_element_type=F32)
    for copy in sends[:4]:
        copy.wait()

    def stencil(x, carry):
        done = []
        for b in range(2):
            here = pl.ds(b * 256 + x * 16, 16)
            acc = pot[x] * xe[b, x + 6] + base[here, :]
            for k in range(1, 7):
                four = (ye[b, x, 8 - k : 24 - k, :] + ye[b, x, 8 + k : 24 + k, :]) + (
                    xe[b, x + 6 - k] + xe[b, x + 6 + k]
                )
                acc = acc + (-0.5 * COEFF[k]) * four
            done.append(acc)
        for b in range(2):
            base[pl.ds(b * 256 + x * 16, 16), :] = done[b]
        return carry

    lax.fori_loop(0, 16, stencil, 0)

    load_cpl.wait()

    for s in range(4):
        for i in range(4):
            cs[pl.ds((s * 4 + i) * 4, 4), :] = cpl_ref[s, i]
    pick = (iota((256, 8), 0) // 32 == iota((256, 8), 1)).astype(F32)
    per_row = lax.dot_general(pick, cs[...], (((1,), (1,)), ((), ())), precision=HI,
                              preferred_element_type=F32)
    r64, c64 = iota((256, 64), 0), iota((256, 64), 1)
    own = ((r64 // 8) % 4 == c64 // 16) & (r64 % 4 == (c64 // 4) % 4)
    per_row = jnp.where(own, per_row, 0.0)
    spread = (iota((64, 256), 0) % 4 == iota((64, 256), 1) % 4).astype(F32)
    wide = lax.dot_general(per_row, spread, (((1,), (0,)), ((), ())), precision=HI,
                           preferred_element_type=F32)
    same = iota((256, 256), 0) // 4 == iota((256, 256), 1) // 4
    atom = iota((256, 256), 0) // 8
    count = jnp.zeros((256, 256), jnp.int32)
    for o in range(8):
        count = jnp.where(atom // 4 == o, cnt_ref[o], count)
    mprime[...] = jnp.where(same & (atom % 4 < count), wide, 0.0)

    for copy in sends[4:]:
        copy.wait()
    far = band(jnp.where(row < 8, row - 8, 120 + row) - col)
    edge = lax.dot_general(zr[...], far, (((0,), (0,)), ((), ())), precision=HI,
                           preferred_element_type=F32)
    base[...] += edge


    for copy in parts:
        copy.wait()

    def got(dx, dy, dz):
        r = recv[slot_of((dx, dy, dz))]
        return r[:, 0:128], r[:, 128:256]

    lane1 = iota((1, 128), 1)
    upper_y, upper_z = (lane1 & 64) != 0, (lane1 & 32) != 0
    halves = []
    for h in range(2):
        by_z = {}
        for dz in (-1, 0, 1):
            by_y = {}
            for dy in (-1, 0, 1):
                by_y[dy] = got(0, dy, dz)[h] + got(1 - 2 * h, dy, dz)[1 - h]
            crossed = jnp.where(upper_y, by_y[1], by_y[-1])
            by_z[dz] = by_y[0] + pltpu.roll(crossed, 64, 1)
        down = pltpu.roll(by_z[1], 96, 1)
        up = pltpu.roll(by_z[-1], 32, 1)
        halves.append(by_z[0] + jnp.where(upper_z, up, down))
    sums = jnp.concatenate(halves, axis=1)
    wrep[...] = exact_dot(mprime[...] * sums, jnp.ones((256, 128), F32), ((1,), (0,)))

    def scatter(o, carry):
        spots, mixes = [], []
        for s in range(4):
            n = o * 4 + s
            for b in range(2):
                mix = jnp.zeros((32, 128), F32)
                for i in range(4):
                    plane = pr[pl.ds(n * 128 + i * 32, 32), :]
                    mix = mix + plane * wrep[pl.ds(n * 8 + b * 4 + i, 1), :]
                mixes.append(mix)
            spots.append(place(o, s))
        for k, mix in enumerate(mixes):
            for yh in range(2):
                zc[(k * 6 + 2 + yh) * 48 + 16 : (k * 6 + 2 + yh) * 48 + 32, :] = mix[yh * 16 : yh * 16 + 16]
        for r in range(8):
            keep = []
            z = (lane - 16 * r) & 127
            for a, b0, c in spots:
                keep.append((z >= c) & (z < c + 16))
            corner = {
                (s, y): ((y - b0) >> 3) * 48 - a
                for s, (a, b0, c) in enumerate(spots) for y in (r, r + 8)
            }
            where = [(b, y, h) for y in (r, r + 8) for b in range(2) for h in range(2)]
            sums = []
            for b, y, h in where:
                acc = sheared[b, y, 8 * h : 8 * h + 8, :]
                for s in range(4):
                    at = (s * 12 + b * 6 + 2) * 48 + 16 + 8 * h
                    w = zc[pl.ds(corner[s, y] + at, 8), :]
                    acc = acc + jnp.where(keep[s], w, 0.0)
                sums.append(acc)
            for (b, y, h), acc in zip(where, sums):
                sheared[b, y, 8 * h : 8 * h + 8, :] = acc
        return carry

    lax.fori_loop(0, 8, scatter, 0)

    outs = []
    for b in range(2):
        planes = [sheared[b, y] for y in range(16)]
        planes = [
            (pltpu.roll(v, 128 - 16 * (y % 8), 1) if y % 8 else v)
            + base[pl.ds(b * 256 + y, 16, stride=16), :]
            for y, v in enumerate(planes)
        ]
        for y, v in enumerate(planes):
            base[pl.ds(b * 256 + y, 16, stride=16), :] = v
        half = pl.ds(b * 256, 256)
        outs.append(pltpu.make_async_copy(base.at[half], out_hbm.at[half], lsem.at[11 + b]))
        outs[b].start()
    for copy in outs:
        copy.wait()


def solution(mesh):
    sizes = tuple(mesh.shape[name] for name in ("gx", "gy", "gz"))
    nslots = 1
    for n in sizes:
        nslots *= len(residues(n))

    def on_device(orbitals, potential, projectors, coupling, block_starts, owner_counts):
        rows = projectors.reshape(32, 4, 32, 128).transpose(0, 2, 1, 3).reshape(4096, 128)
        matrices = coupling.reshape(8, 4, 4, 4).transpose(1, 2, 3, 0)
        starts = block_starts.reshape(8, 4, 3).transpose(2, 1, 0)
        counts = owner_counts.reshape(8)
        hbm = pl.BlockSpec(memory_space=pltpu.HBM)
        return pl.pallas_call(
            functools.partial(kernel, sizes),
            out_shape=jax.ShapeDtypeStruct((512, 128), F32),
            in_specs=[hbm] * 6,
            out_specs=hbm,
            scratch_shapes=[
                pltpu.VMEM((512, 128), F32),
                pltpu.VMEM((4608, 128), F32),
                pltpu.VMEM((2, 28, 16, 128), F32),
                pltpu.VMEM((2, 16, 32, 128), F32),
                pltpu.VMEM((16, 16, 128), F32),
                pltpu.VMEM((4096, 128), F32),
                pltpu.VMEM((4096, 128), F32),
                pltpu.VMEM((2, 16, 16, 128), F32),
                pltpu.VMEM((2048, 128), F32),
                pltpu.VMEM((16, 512), F32),
                pltpu.VMEM((16, 512), F32),
                pltpu.VMEM((nslots, 1, 256), F32),
                pltpu.VMEM((2304, 128), F32),
                pltpu.VMEM((256, 128), F32),
                pltpu.VMEM((64, 8), F32),
                pltpu.VMEM((256, 256), F32),
                pltpu.VMEM((512, 128), F32),
                pltpu.VMEM((4, 4, 4, 8), F32),
                pltpu.SMEM((3, 4, 8), jnp.int32),
                pltpu.SMEM((8,), jnp.int32),
                pltpu.SemaphoreType.DMA((13,)),
                pltpu.SemaphoreType.DMA((6,)),
                pltpu.SemaphoreType.DMA((6,)),
                pltpu.SemaphoreType.DMA((nslots,)),
                pltpu.SemaphoreType.DMA((nslots,)),
            ],
            compiler_params=pltpu.CompilerParams(
                collective_id=0, has_side_effects=True, vmem_limit_bytes=60 * 1024 * 1024
            ),
        )(orbitals, potential, rows, matrices, starts, counts).reshape(2, 16, 16, 128)

    in_specs = (
        P(None, "gx", "gy", "gz"),
        P("gx", "gy", "gz"),
        P("gx", "gy", "gz", None, None, None, None),
        P("gx", "gy", "gz", None, None, None, None),
        P("gx", "gy", "gz", None, None, None),
        P("gx", "gy", "gz", None),
    )
    return jax.shard_map(
        on_device, mesh=mesh, in_specs=in_specs,
        out_specs=P(None, "gx", "gy", "gz"), check_vma=False,
    )
```

```python
import functools

import jax
import jax.numpy as jnp
from jax import lax
from jax.experimental import pallas as pl
from jax.experimental.pallas import tpu as pltpu
from jax.sharding import PartitionSpec as P

MESH = pl.DeviceIdType.MESH
HI = lax.Precision.HIGHEST
F32 = jnp.float32
COEFF = [
    -5369.0 / 1800.0,
    12.0 / 7.0,
    -15.0 / 56.0,
    10.0 / 189.0,
    -1.0 / 112.0,
    2.0 / 1925.0,
    -1.0 / 16632.0,
]


def iota(shape, dim):
    return lax.broadcasted_iota(jnp.int32, shape, dim)


def band(distance):
    d = jnp.abs(distance)
    out = jnp.zeros(distance.shape, F32)
    for k in range(1, 7):
        out = jnp.where(d == k, -0.5 * COEFF[k], out)
    return out


def split3(v):
    hi = v.astype(jnp.bfloat16)
    left = v - hi.astype(F32)
    mid = left.astype(jnp.bfloat16)
    low = (left - mid.astype(F32)).astype(jnp.bfloat16)
    return hi, mid, low


def exact_dot(v, units, dims, flip=False):
    units = units.astype(jnp.bfloat16)
    total = None
    for term in reversed(split3(v)):
        pair = (units, term) if flip else (term, units)
        out = lax.dot_general(*pair, (dims, ((), ())), preferred_element_type=F32)
        total = out if total is None else total + out
    return total


def residues(n):
    return [0, 1] if n == 2 else [0, 1, n - 1]


def kernel(
    sizes,
    x_hbm, pot_hbm, p_hbm, cpl_hbm, st_hbm, cnt_hbm,
    out_hbm,
    base, xt, xe, ye, pot, pv, pr, sheared, accs, zs, zr, recv, zc, wrep, cs, mprime, fold,
    cpl_ref, st_ref, cnt_ref,
    lsem, hsend, hrecv, psend, precv,
):
    names = ("gx", "gy", "gz")
    me = [lax.axis_index(name) for name in names]
    res = [residues(n) for n in sizes]
    slots = {}
    for ex in res[0]:
        for ey in res[1]:
            for ez in res[2]:
                slots[(ex, ey, ez)] = len(slots)

    near_by = []
    for d in range(3):
        up = jnp.where(me[d] == sizes[d] - 1, 0, me[d] + 1)
        down = jnp.where(me[d] == 0, sizes[d] - 1, me[d] - 1)
        near_by.append({0: me[d], sizes[d] - 1: down, 1: up})

    def device(offset):
        return tuple(near_by[d][offset[d] % sizes[d]] for d in range(3))

    def slot_of(offset):
        return slots[tuple(offset[d] % sizes[d] for d in range(3))]

    load_x = pltpu.make_async_copy(x_hbm, xe.at[:, 6:22], lsem.at[0])
    load_y = pltpu.make_async_copy(x_hbm, ye.at[:, :, 8:24], lsem.at[1])
    load_p = [
        pltpu.make_async_copy(p_hbm.at[pl.ds(k * 2048, 2048)], pv.at[pl.ds(k * 2048, 2048)],
                              lsem.at[7 + k])
        for k in range(2)
    ]
    load_pot = pltpu.make_async_copy(pot_hbm, pot, lsem.at[3])
    load_st = pltpu.make_async_copy(st_hbm, st_ref, lsem.at[4])
    load_cnt = pltpu.make_async_copy(cnt_hbm, cnt_ref, lsem.at[5])
    load_cpl = pltpu.make_async_copy(cpl_hbm, cpl_ref, lsem.at[6])
    load_st.start()
    for copy in load_p:
        copy.start()
    load_x.start()
    load_cpl.start()
    load_cnt.start()
    load_y.start()
    load_pot.start()

    barrier = pltpu.get_barrier_semaphore()
    others = [e for e in slots if e != (0, 0, 0)]
    others.sort(key=lambda e: -sum(e))
    for e in others:
        pl.semaphore_signal(barrier, inc=1, device_id=device(e), device_id_type=MESH)

    def clear(i, carry):
        for b in range(2):
            xt[b, i] = jnp.zeros((48, 128), F32)
        return carry

    lax.fori_loop(0, 48, clear, 0)

    def clear_mix(i, carry):
        zc[pl.ds(i * 96, 96), :] = jnp.zeros((96, 128), F32)
        return carry

    lax.fori_loop(0, 24, clear_mix, 0)

    def clear_sum(i, carry):
        for b in range(2):
            sheared[b, i] = jnp.zeros((16, 128), F32)
        return carry

    lax.fori_loop(0, 16, clear_sum, 0)

    lane = iota((8, 128), 1)

    def place(o, s):
        a = st_ref[0, s, o] - 16 * (o >> 2)
        b0 = st_ref[1, s, o] - 16 * ((o >> 1) & 1)
        c = st_ref[2, s, o] - 128 * (o & 1)
        return a, b0, c

    load_x.wait()

    fold[...] = xe[:, 6:22].reshape(512, 128)
    for b in range(2):
        planes = [fold[pl.ds(b * 256 + y, 16, stride=16), :] for y in range(16)]
        planes = [pltpu.roll(v, 16 * (y % 8), 1) if y % 8 else v for y, v in enumerate(planes)]
        for y, v in enumerate(planes):
            xt[b, 16 + y, 16:32, :] = v

    row, col = iota((16, 128), 0), iota((16, 128), 1)
    sel = (col == jnp.where(row < 8, 120 + row, row - 8)).astype(F32)
    zs[...] = exact_dot(fold[...], sel, ((1,), (1,)), flip=True)
    pl.semaphore_wait(barrier, len(others))

    sends = []

    def send(src, dst, k, offset):
        copy = pltpu.make_async_remote_copy(
            src_ref=src, dst_ref=dst, send_sem=hsend.at[k], recv_sem=hrecv.at[k],
            device_id=device(offset), device_id_type=MESH,
        )
        copy.start()
        sends.append(copy)

    send(x_hbm.at[:, :, 8:16, :], ye.at[:, :, 0:8, :], 0, (0, 1, 0))
    send(x_hbm.at[:, :, 0:8, :], ye.at[:, :, 24:32, :], 1, (0, -1, 0))
    send(x_hbm.at[:, 10:16], xe.at[:, 0:6], 2, (1, 0, 0))
    send(x_hbm.at[:, 0:6], xe.at[:, 22:28], 3, (-1, 0, 0))
    send(zs.at[0:8], zr.at[0:8], 4, (0, 0, 1))
    send(zs.at[8:16], zr.at[8:16], 5, (0, 0, -1))

    load_st.wait()
    load_cnt.wait()

    def gather(n, carry):
        a, b0, c = place(n >> 2, n & 3)
        slabs = [
            xt[b, pl.ds(16 + b0, 16), pl.ds(16 + a, 16), :] for b in range(2)
        ]
        first = lane - 16 * b0
        parts = [(b, yh, h) for b in range(2) for yh in range(2) for h in range(2)]
        packed = {k: jnp.zeros((8, 128), F32) for k in parts}
        for y in range(8):
            z = (first - 16 * y) & 127
            keep = (z >= c) & (z < c + 16)
            for b, yh, h in parts:
                w = slabs[b][8 * yh + y, 8 * h : 8 * h + 8]
                packed[b, yh, h] = jnp.where(keep, w, packed[b, yh, h])
        by = (c + 16 * b0) & 127
        for i in range(4):
            acc = [None, None]
            for yh in range(2):
                plane = pltpu.roll(pv[pl.ds(n * 128 + yh * 4 + i, 16, stride=8), :], by, 1)
                pr[pl.ds(n * 128 + i * 32 + yh * 16, 16), :] = plane
                for b in range(2):
                    term = (packed[b, yh, 0] * plane[0:8]) + (packed[b, yh, 1] * plane[8:16])
                    acc[b] = term if acc[b] is None else acc[b] + term
            for b in range(2):
                accs[pl.ds(n * 64 + (b * 4 + i) * 8, 8), :] = acc[b]
        return carry

    for k in range(2):
        load_p[k].wait()
        lax.fori_loop(16 * k, 16 * k + 16, gather, 0)

    total = accs[pl.ds(0, 256, stride=8), :]
    for k in range(1, 8):
        total = total + accs[pl.ds(k, 256, stride=8), :]
    mine = exact_dot(total, jnp.ones((8, 128), F32), ((1,), (1,)), flip=True)
    recv[0] = mine[0:1]
    parts = []
    for k, e in enumerate(others):
        copy = pltpu.make_async_remote_copy(
            src_ref=recv.at[0], dst_ref=recv.at[slot_of(tuple(-v for v in e))],
            send_sem=psend.at[k], recv_sem=precv.at[slot_of(tuple(-v for v in e))],
            device_id=device(e), device_id_type=MESH,
        )
        copy.start()
        parts.append(copy)

    load_y.wait()
    load_pot.wait()
    r128, c128 = iota((128, 128), 0), iota((128, 128), 1)
    near = jnp.where(r128 == c128, -0.5 * 3.0 * COEFF[0], band(r128 - c128))
    base[...] = lax.dot_general(fold[...], near, (((1,), (0,)), ((), ())), precision=HI,
                           preferred_element_type=F32)
    for copy in sends[:4]:
        copy.wait()

    def stencil(x, carry):
        done = []
        for b in range(2):
            here = pl.ds(b * 256 + x * 16, 16)
            acc = pot[x] * xe[b, x + 6] + base[here, :]
            for k in range(1, 7):
                four = (ye[b, x, 8 - k : 24 - k, :] + ye[b, x, 8 + k : 24 + k, :]) + (
                    xe[b, x + 6 - k] + xe[b, x + 6 + k]
                )
                acc = acc + (-0.5 * COEFF[k]) * four
            done.append(acc)
        for b in range(2):
            base[pl.ds(b * 256 + x * 16, 16), :] = done[b]
        return carry

    lax.fori_loop(0, 16, stencil, 0)

    load_cpl.wait()

    for s in range(4):
        for i in range(4):
            cs[pl.ds((s * 4 + i) * 4, 4), :] = cpl_ref[s, i]
    pick = (iota((8, 256), 0) == iota((8, 256), 1) // 32).astype(F32)
    spread = exact_dot(cs[...], pick, ((1,), (0,)))
    r64, c64 = iota((64, 256), 0), iota((64, 256), 1)
    own = (r64 // 16 == (c64 // 8) % 4) & (r64 % 4 == c64 % 4)
    spread = jnp.where(own, spread, 0.0)
    rows_of = (iota((8, 64), 0) % 4 == (iota((8, 64), 1) // 4) % 4).astype(F32)
    by_lane = exact_dot(spread, rows_of, ((1,), (0,)), flip=True)
    lane8 = iota((8, 256), 1)
    count = jnp.zeros((8, 256), jnp.int32)
    for o in range(8):
        count = jnp.where(lane8 // 32 == o, cnt_ref[o], count)
    mprime[...] = jnp.where((lane8 // 8) % 4 < count, by_lane, 0.0)

    for copy in sends[4:]:
        copy.wait()
    far = band(jnp.where(row < 8, row - 8, 120 + row) - col)
    edge = lax.dot_general(zr[...], far, (((0,), (0,)), ((), ())), precision=HI,
                           preferred_element_type=F32)
    base[...] += edge


    for copy in parts:
        copy.wait()

    def got(dx, dy, dz):
        r = recv[slot_of((dx, dy, dz))]
        return r[:, 0:128], r[:, 128:256]

    lane1 = iota((1, 128), 1)
    upper_y, upper_z = (lane1 & 64) != 0, (lane1 & 32) != 0
    halves = []
    for h in range(2):
        by_z = {}
        for dz in (-1, 0, 1):
            by_y = {}
            for dy in (-1, 0, 1):
                by_y[dy] = got(0, dy, dz)[h] + got(1 - 2 * h, dy, dz)[1 - h]
            crossed = jnp.where(upper_y, by_y[1], by_y[-1])
            by_z[dz] = by_y[0] + pltpu.roll(crossed, 64, 1)
        down = pltpu.roll(by_z[1], 96, 1)
        up = pltpu.roll(by_z[-1], 32, 1)
        halves.append(by_z[0] + jnp.where(upper_z, up, down))
    for h in range(2):
        v = mprime[:, 128 * h : 128 * h + 128] * halves[h]
        v = v + pltpu.roll(v, 127, 1)
        v = v + pltpu.roll(v, 126, 1)
        for g in range(32):
            wrep[(h * 32 + g) * 8 : (h * 32 + g) * 8 + 8, :] = jnp.broadcast_to(
                v[:, 4 * g : 4 * g + 1], (8, 128)
            )

    def scatter(o, carry):
        spots = []
        for s in range(4):
            n = o * 4 + s
            planes = pr[pl.ds(n * 128, 128), :]
            for b in range(2):
                mix = None
                for i in range(4):
                    term = planes[i * 32 : i * 32 + 32] * wrep[pl.ds(n * 16 + b * 8 + i, 1), :]
                    mix = term if mix is None else mix + term
                for yh in range(2):
                    at = (s * 12 + b * 6 + 2 + yh) * 48 + 16
                    zc[at : at + 16, :] = mix[yh * 16 : yh * 16 + 16]
            spots.append(place(o, s))
        for r in range(8):
            keep = []
            z = (lane - 16 * r) & 127
            for a, b0, c in spots:
                keep.append((z >= c) & (z < c + 16))
            corner = {
                (s, y): ((y - b0) >> 3) * 48 - a
                for s, (a, b0, c) in enumerate(spots) for y in (r, r + 8)
            }
            where = [(b, y, h) for y in (r, r + 8) for b in range(2) for h in range(2)]
            sums = []
            for b, y, h in where:
                acc = sheared[b, y, 8 * h : 8 * h + 8, :]
                for s in range(4):
                    at = (s * 12 + b * 6 + 2) * 48 + 16 + 8 * h
                    w = zc[pl.ds(corner[s, y] + at, 8), :]
                    acc = acc + jnp.where(keep[s], w, 0.0)
                sums.append(acc)
            for (b, y, h), acc in zip(where, sums):
                sheared[b, y, 8 * h : 8 * h + 8, :] = acc
        return carry

    lax.fori_loop(0, 8, scatter, 0)

    outs = []
    for b in range(2):
        planes = [sheared[b, y] for y in range(16)]
        planes = [
            (pltpu.roll(v, 128 - 16 * (y % 8), 1) if y % 8 else v)
            + base[pl.ds(b * 256 + y, 16, stride=16), :]
            for y, v in enumerate(planes)
        ]
        for y, v in enumerate(planes):
            base[pl.ds(b * 256 + y, 16, stride=16), :] = v
        half = pl.ds(b * 256, 256)
        outs.append(pltpu.make_async_copy(base.at[half], out_hbm.at[half], lsem.at[11 + b]))
        outs[b].start()
    for copy in outs:
        copy.wait()


def solution(mesh):
    sizes = tuple(mesh.shape[name] for name in ("gx", "gy", "gz"))
    nslots = 1
    for n in sizes:
        nslots *= len(residues(n))

    def on_device(orbitals, potential, projectors, coupling, block_starts, owner_counts):
        rows = projectors.reshape(32, 4, 32, 128).transpose(0, 2, 1, 3).reshape(4096, 128)
        matrices = coupling.reshape(8, 4, 4, 4).transpose(1, 2, 3, 0)
        starts = block_starts.reshape(8, 4, 3).transpose(2, 1, 0)
        counts = owner_counts.reshape(8)
        hbm = pl.BlockSpec(memory_space=pltpu.HBM)
        return pl.pallas_call(
            functools.partial(kernel, sizes),
            out_shape=jax.ShapeDtypeStruct((512, 128), F32),
            in_specs=[hbm] * 6,
            out_specs=hbm,
            scratch_shapes=[
                pltpu.VMEM((512, 128), F32),
                pltpu.VMEM((2, 48, 48, 128), F32),
                pltpu.VMEM((2, 28, 16, 128), F32),
                pltpu.VMEM((2, 16, 32, 128), F32),
                pltpu.VMEM((16, 16, 128), F32),
                pltpu.VMEM((4096, 128), F32),
                pltpu.VMEM((4096, 128), F32),
                pltpu.VMEM((2, 16, 16, 128), F32),
                pltpu.VMEM((2048, 128), F32),
                pltpu.VMEM((16, 512), F32),
                pltpu.VMEM((16, 512), F32),
                pltpu.VMEM((nslots, 1, 256), F32),
                pltpu.VMEM((2304, 128), F32),
                pltpu.VMEM((512, 128), F32),
                pltpu.VMEM((64, 8), F32),
                pltpu.VMEM((8, 256), F32),
                pltpu.VMEM((512, 128), F32),
                pltpu.VMEM((4, 4, 4, 8), F32),
                pltpu.SMEM((3, 4, 8), jnp.int32),
                pltpu.SMEM((8,), jnp.int32),
                pltpu.SemaphoreType.DMA((13,)),
                pltpu.SemaphoreType.DMA((6,)),
                pltpu.SemaphoreType.DMA((6,)),
                pltpu.SemaphoreType.DMA((nslots,)),
                pltpu.SemaphoreType.DMA((nslots,)),
            ],
            compiler_params=pltpu.CompilerParams(
                collective_id=0, has_side_effects=True, vmem_limit_bytes=60 * 1024 * 1024
            ),
        )(orbitals, potential, rows, matrices, starts, counts).reshape(2, 16, 16, 128)

    in_specs = (
        P(None, "gx", "gy", "gz"),
        P("gx", "gy", "gz"),
        P("gx", "gy", "gz", None, None, None, None),
        P("gx", "gy", "gz", None, None, None, None),
        P("gx", "gy", "gz", None, None, None),
        P("gx", "gy", "gz", None),
    )
    return jax.shard_map(
        on_device, mesh=mesh, in_specs=in_specs,
        out_specs=P(None, "gx", "gy", "gz"), check_vma=False,
    )
```

```python
import functools

import jax
import jax.numpy as jnp
from jax import lax
from jax.experimental import pallas as pl
from jax.experimental.pallas import tpu as pltpu
from jax.sharding import PartitionSpec as P

MESH = pl.DeviceIdType.MESH
HI = lax.Precision.HIGHEST
F32 = jnp.float32
COEFF = [
    -5369.0 / 1800.0,
    12.0 / 7.0,
    -15.0 / 56.0,
    10.0 / 189.0,
    -1.0 / 112.0,
    2.0 / 1925.0,
    -1.0 / 16632.0,
]


def iota(shape, dim):
    return lax.broadcasted_iota(jnp.int32, shape, dim)


def band(distance):
    d = jnp.abs(distance)
    out = jnp.zeros(distance.shape, F32)
    for k in range(1, 7):
        out = jnp.where(d == k, -0.5 * COEFF[k], out)
    return out


def split3(v):
    hi = v.astype(jnp.bfloat16)
    left = v - hi.astype(F32)
    mid = left.astype(jnp.bfloat16)
    low = (left - mid.astype(F32)).astype(jnp.bfloat16)
    return hi, mid, low


def exact_dot(v, units, dims, flip=False):
    units = units.astype(jnp.bfloat16)
    total = None
    for term in reversed(split3(v)):
        pair = (units, term) if flip else (term, units)
        out = lax.dot_general(*pair, (dims, ((), ())), preferred_element_type=F32)
        total = out if total is None else total + out
    return total


def residues(n):
    return [0, 1] if n == 2 else [0, 1, n - 1]


def kernel(
    sizes,
    x_hbm, pot_hbm, p_hbm, cpl_hbm, st_hbm, cnt_hbm,
    out_hbm,
    base, xt, xe, ye, pot, pv, pr, sheared, accs, zs, zr, recv, zc, wrep, cs, mprime, fold,
    cpl_ref, st_ref, cnt_ref,
    lsem, hsend, hrecv, psend, precv,
):
    names = ("gx", "gy", "gz")
    me = [lax.axis_index(name) for name in names]
    res = [residues(n) for n in sizes]
    slots = {}
    for ex in res[0]:
        for ey in res[1]:
            for ez in res[2]:
                slots[(ex, ey, ez)] = len(slots)

    near_by = []
    for d in range(3):
        up = jnp.where(me[d] == sizes[d] - 1, 0, me[d] + 1)
        down = jnp.where(me[d] == 0, sizes[d] - 1, me[d] - 1)
        near_by.append({0: me[d], sizes[d] - 1: down, 1: up})

    def device(offset):
        return tuple(near_by[d][offset[d] % sizes[d]] for d in range(3))

    def slot_of(offset):
        return slots[tuple(offset[d] % sizes[d] for d in range(3))]

    load_x = pltpu.make_async_copy(x_hbm, xe.at[:, 6:22], lsem.at[0])
    load_y = pltpu.make_async_copy(x_hbm, ye.at[:, :, 8:24], lsem.at[1])
    load_p = [
        pltpu.make_async_copy(p_hbm.at[pl.ds(k * 2048, 2048)], pv.at[pl.ds(k * 2048, 2048)],
                              lsem.at[7 + k])
        for k in range(2)
    ]
    load_pot = pltpu.make_async_copy(pot_hbm, pot, lsem.at[3])
    load_st = pltpu.make_async_copy(st_hbm, st_ref, lsem.at[4])
    load_cnt = pltpu.make_async_copy(cnt_hbm, cnt_ref, lsem.at[5])
    load_cpl = pltpu.make_async_copy(cpl_hbm, cpl_ref, lsem.at[6])
    load_st.start()
    for copy in load_p:
        copy.start()
    load_x.start()
    load_cpl.start()
    load_cnt.start()
    load_y.start()
    load_pot.start()

    barrier = pltpu.get_barrier_semaphore()
    others = [e for e in slots if e != (0, 0, 0)]
    others.sort(key=lambda e: -sum(e))
    for e in others:
        pl.semaphore_signal(barrier, inc=1, device_id=device(e), device_id_type=MESH)

    pl.semaphore_wait(barrier, len(others))

    sends = []

    def send(src, dst, k, offset):
        copy = pltpu.make_async_remote_copy(
            src_ref=src, dst_ref=dst, send_sem=hsend.at[k], recv_sem=hrecv.at[k],
            device_id=device(offset), device_id_type=MESH,
        )
        copy.start()
        sends.append(copy)

    send(x_hbm.at[:, :, 8:16, :], ye.at[:, :, 0:8, :], 0, (0, 1, 0))
    send(x_hbm.at[:, :, 0:8, :], ye.at[:, :, 24:32, :], 1, (0, -1, 0))
    send(x_hbm.at[:, 10:16], xe.at[:, 0:6], 2, (1, 0, 0))
    send(x_hbm.at[:, 0:6], xe.at[:, 22:28], 3, (-1, 0, 0))
    def clear(i, carry):
        for b in range(2):
            xt[b, i] = jnp.zeros((48, 128), F32)
        return carry

    lax.fori_loop(0, 48, clear, 0)

    def clear_mix(i, carry):
        zc[pl.ds(i * 96, 96), :] = jnp.zeros((96, 128), F32)
        return carry

    lax.fori_loop(0, 24, clear_mix, 0)

    def clear_sum(i, carry):
        for b in range(2):
            sheared[b, i] = jnp.zeros((16, 128), F32)
        return carry

    lax.fori_loop(0, 16, clear_sum, 0)

    lane = iota((8, 128), 1)

    def place(o, s):
        a = st_ref[0, s, o] - 16 * (o >> 2)
        b0 = st_ref[1, s, o] - 16 * ((o >> 1) & 1)
        c = st_ref[2, s, o] - 128 * (o & 1)
        return a, b0, c

    load_x.wait()

    fold[...] = xe[:, 6:22].reshape(512, 128)
    for b in range(2):
        planes = [fold[pl.ds(b * 256 + y, 16, stride=16), :] for y in range(16)]
        planes = [pltpu.roll(v, 16 * (y % 8), 1) if y % 8 else v for y, v in enumerate(planes)]
        for y, v in enumerate(planes):
            xt[b, 16 + y, 16:32, :] = v

    row, col = iota((16, 128), 0), iota((16, 128), 1)
    sel = (col == jnp.where(row < 8, 120 + row, row - 8)).astype(F32)
    zs[...] = exact_dot(fold[...], sel, ((1,), (1,)), flip=True)
    send(zs.at[0:8], zr.at[0:8], 4, (0, 0, 1))
    send(zs.at[8:16], zr.at[8:16], 5, (0, 0, -1))

    load_st.wait()
    load_cnt.wait()

    def gather(n, carry):
        a, b0, c = place(n >> 2, n & 3)
        slabs = [
            xt[b, pl.ds(16 + b0, 16), pl.ds(16 + a, 16), :] for b in range(2)
        ]
        first = lane - 16 * b0
        parts = [(b, yh, h) for b in range(2) for yh in range(2) for h in range(2)]
        packed = {k: jnp.zeros((8, 128), F32) for k in parts}
        for y in range(8):
            z = (first - 16 * y) & 127
            keep = (z >= c) & (z < c + 16)
            for b, yh, h in parts:
                w = slabs[b][8 * yh + y, 8 * h : 8 * h + 8]
                packed[b, yh, h] = jnp.where(keep, w, packed[b, yh, h])
        by = (c + 16 * b0) & 127
        for i in range(4):
            acc = [None, None]
            for yh in range(2):
                plane = pltpu.roll(pv[pl.ds(n * 128 + yh * 4 + i, 16, stride=8), :], by, 1)
                pr[pl.ds(n * 128 + i * 32 + yh * 16, 16), :] = plane
                for b in range(2):
                    term = (packed[b, yh, 0] * plane[0:8]) + (packed[b, yh, 1] * plane[8:16])
                    acc[b] = term if acc[b] is None else acc[b] + term
            for b in range(2):
                accs[pl.ds(n * 64 + (b * 4 + i) * 8, 8), :] = acc[b]
        return carry

    for k in range(2):
        load_p[k].wait()
        lax.fori_loop(16 * k, 16 * k + 16, gather, 0)

    total = accs[pl.ds(0, 256, stride=8), :]
    for k in range(1, 8):
        total = total + accs[pl.ds(k, 256, stride=8), :]
    mine = exact_dot(total, jnp.ones((8, 128), F32), ((1,), (1,)), flip=True)
    recv[0] = mine[0:1]
    parts = []
    for k, e in enumerate(others):
        copy = pltpu.make_async_remote_copy(
            src_ref=recv.at[0], dst_ref=recv.at[slot_of(tuple(-v for v in e))],
            send_sem=psend.at[k], recv_sem=precv.at[slot_of(tuple(-v for v in e))],
            device_id=device(e), device_id_type=MESH,
        )
        copy.start()
        parts.append(copy)

    load_y.wait()
    load_pot.wait()
    r128, c128 = iota((128, 128), 0), iota((128, 128), 1)
    near = jnp.where(r128 == c128, -0.5 * 3.0 * COEFF[0], band(r128 - c128))
    base[...] = lax.dot_general(fold[...], near, (((1,), (0,)), ((), ())), precision=HI,
                           preferred_element_type=F32)
    for copy in sends[:4]:
        copy.wait()

    def stencil(x, carry):
        done = []
        for b in range(2):
            here = pl.ds(b * 256 + x * 16, 16)
            acc = pot[x] * xe[b, x + 6] + base[here, :]
            for k in range(1, 7):
                four = (ye[b, x, 8 - k : 24 - k, :] + ye[b, x, 8 + k : 24 + k, :]) + (
                    xe[b, x + 6 - k] + xe[b, x + 6 + k]
                )
                acc = acc + (-0.5 * COEFF[k]) * four
            done.append(acc)
        for b in range(2):
            base[pl.ds(b * 256 + x * 16, 16), :] = done[b]
        return carry

    lax.fori_loop(0, 16, stencil, 0)

    load_cpl.wait()

    for s in range(4):
        for i in range(4):
            cs[pl.ds((s * 4 + i) * 4, 4), :] = cpl_ref[s, i]
    pick = (iota((8, 256), 0) == iota((8, 256), 1) // 32).astype(F32)
    spread = exact_dot(cs[...], pick, ((1,), (0,)))
    r64, c64 = iota((64, 256), 0), iota((64, 256), 1)
    own = (r64 // 16 == (c64 // 8) % 4) & (r64 % 4 == c64 % 4)
    spread = jnp.where(own, spread, 0.0)
    rows_of = (iota((8, 64), 0) % 4 == (iota((8, 64), 1) // 4) % 4).astype(F32)
    by_lane = exact_dot(spread, rows_of, ((1,), (0,)), flip=True)
    lane8 = iota((8, 256), 1)
    count = jnp.zeros((8, 256), jnp.int32)
    for o in range(8):
        count = jnp.where(lane8 // 32 == o, cnt_ref[o], count)
    mprime[...] = jnp.where((lane8 // 8) % 4 < count, by_lane, 0.0)

    for copy in sends[4:]:
        copy.wait()
    far = band(jnp.where(row < 8, row - 8, 120 + row) - col)
    edge = lax.dot_general(zr[...], far, (((0,), (0,)), ((), ())), precision=HI,
                           preferred_element_type=F32)
    base[...] += edge


    for copy in parts:
        copy.wait()

    def got(dx, dy, dz):
        r = recv[slot_of((dx, dy, dz))]
        return r[:, 0:128], r[:, 128:256]

    lane1 = iota((1, 128), 1)
    upper_y, upper_z = (lane1 & 64) != 0, (lane1 & 32) != 0
    halves = []
    for h in range(2):
        by_z = {}
        for dz in (-1, 0, 1):
            by_y = {}
            for dy in (-1, 0, 1):
                by_y[dy] = got(0, dy, dz)[h] + got(1 - 2 * h, dy, dz)[1 - h]
            crossed = jnp.where(upper_y, by_y[1], by_y[-1])
            by_z[dz] = by_y[0] + pltpu.roll(crossed, 64, 1)
        down = pltpu.roll(by_z[1], 96, 1)
        up = pltpu.roll(by_z[-1], 32, 1)
        halves.append(by_z[0] + jnp.where(upper_z, up, down))
    for h in range(2):
        v = mprime[:, 128 * h : 128 * h + 128] * halves[h]
        v = v + pltpu.roll(v, 127, 1)
        v = v + pltpu.roll(v, 126, 1)
        for g in range(32):
            wrep[(h * 32 + g) * 8 : (h * 32 + g) * 8 + 8, :] = jnp.broadcast_to(
                v[:, 4 * g : 4 * g + 1], (8, 128)
            )

    def scatter(o, carry):
        spots = []
        for s in range(4):
            n = o * 4 + s
            planes = pr[pl.ds(n * 128, 128), :]
            for b in range(2):
                mix = None
                for i in range(4):
                    term = planes[i * 32 : i * 32 + 32] * wrep[pl.ds(n * 16 + b * 8 + i, 1), :]
                    mix = term if mix is None else mix + term
                for yh in range(2):
                    at = (s * 12 + b * 6 + 2 + yh) * 48 + 16
                    zc[at : at + 16, :] = mix[yh * 16 : yh * 16 + 16]
            spots.append(place(o, s))
        for r in range(8):
            keep = []
            z = (lane - 16 * r) & 127
            for a, b0, c in spots:
                keep.append((z >= c) & (z < c + 16))
            corner = {
                (s, y): ((y - b0) >> 3) * 48 - a
                for s, (a, b0, c) in enumerate(spots) for y in (r, r + 8)
            }
            where = [(b, y, h) for y in (r, r + 8) for b in range(2) for h in range(2)]
            sums = []
            for b, y, h in where:
                acc = sheared[b, y, 8 * h : 8 * h + 8, :]
                for s in range(4):
                    at = (s * 12 + b * 6 + 2) * 48 + 16 + 8 * h
                    w = zc[pl.ds(corner[s, y] + at, 8), :]
                    acc = acc + jnp.where(keep[s], w, 0.0)
                sums.append(acc)
            for (b, y, h), acc in zip(where, sums):
                sheared[b, y, 8 * h : 8 * h + 8, :] = acc
        return carry

    lax.fori_loop(0, 8, scatter, 0)

    outs = []
    for b in range(2):
        planes = [sheared[b, y] for y in range(16)]
        planes = [
            (pltpu.roll(v, 128 - 16 * (y % 8), 1) if y % 8 else v)
            + base[pl.ds(b * 256 + y, 16, stride=16), :]
            for y, v in enumerate(planes)
        ]
        for y, v in enumerate(planes):
            base[pl.ds(b * 256 + y, 16, stride=16), :] = v
        half = pl.ds(b * 256, 256)
        outs.append(pltpu.make_async_copy(base.at[half], out_hbm.at[half], lsem.at[11 + b]))
        outs[b].start()
    for copy in outs:
        copy.wait()


def solution(mesh):
    sizes = tuple(mesh.shape[name] for name in ("gx", "gy", "gz"))
    nslots = 1
    for n in sizes:
        nslots *= len(residues(n))

    def on_device(orbitals, potential, projectors, coupling, block_starts, owner_counts):
        rows = projectors.reshape(32, 4, 32, 128).transpose(0, 2, 1, 3).reshape(4096, 128)
        matrices = coupling.reshape(8, 4, 4, 4).transpose(1, 2, 3, 0)
        starts = block_starts.reshape(8, 4, 3).transpose(2, 1, 0)
        counts = owner_counts.reshape(8)
        hbm = pl.BlockSpec(memory_space=pltpu.HBM)
        return pl.pallas_call(
            functools.partial(kernel, sizes),
            out_shape=jax.ShapeDtypeStruct((512, 128), F32),
            in_specs=[hbm] * 6,
            out_specs=hbm,
            scratch_shapes=[
                pltpu.VMEM((512, 128), F32),
                pltpu.VMEM((2, 48, 48, 128), F32),
                pltpu.VMEM((2, 28, 16, 128), F32),
                pltpu.VMEM((2, 16, 32, 128), F32),
                pltpu.VMEM((16, 16, 128), F32),
                pltpu.VMEM((4096, 128), F32),
                pltpu.VMEM((4096, 128), F32),
                pltpu.VMEM((2, 16, 16, 128), F32),
                pltpu.VMEM((2048, 128), F32),
                pltpu.VMEM((16, 512), F32),
                pltpu.VMEM((16, 512), F32),
                pltpu.VMEM((nslots, 1, 256), F32),
                pltpu.VMEM((2304, 128), F32),
                pltpu.VMEM((512, 128), F32),
                pltpu.VMEM((64, 8), F32),
                pltpu.VMEM((8, 256), F32),
                pltpu.VMEM((512, 128), F32),
                pltpu.VMEM((4, 4, 4, 8), F32),
                pltpu.SMEM((3, 4, 8), jnp.int32),
                pltpu.SMEM((8,), jnp.int32),
                pltpu.SemaphoreType.DMA((13,)),
                pltpu.SemaphoreType.DMA((6,)),
                pltpu.SemaphoreType.DMA((6,)),
                pltpu.SemaphoreType.DMA((nslots,)),
                pltpu.SemaphoreType.DMA((nslots,)),
            ],
            compiler_params=pltpu.CompilerParams(
                collective_id=0, has_side_effects=True, vmem_limit_bytes=60 * 1024 * 1024
            ),
        )(orbitals, potential, rows, matrices, starts, counts).reshape(2, 16, 16, 128)

    in_specs = (
        P(None, "gx", "gy", "gz"),
        P("gx", "gy", "gz"),
        P("gx", "gy", "gz", None, None, None, None),
        P("gx", "gy", "gz", None, None, None, None),
        P("gx", "gy", "gz", None, None, None),
        P("gx", "gy", "gz", None),
    )
    return jax.shard_map(
        on_device, mesh=mesh, in_specs=in_specs,
        out_specs=P(None, "gx", "gy", "gz"), check_vma=False,
    )
```

```python
import functools

import jax
import jax.numpy as jnp
from jax import lax
from jax.experimental import pallas as pl
from jax.experimental.pallas import tpu as pltpu
from jax.sharding import PartitionSpec as P

MESH = pl.DeviceIdType.MESH
HI = lax.Precision.HIGHEST
F32 = jnp.float32
COEFF = [
    -5369.0 / 1800.0,
    12.0 / 7.0,
    -15.0 / 56.0,
    10.0 / 189.0,
    -1.0 / 112.0,
    2.0 / 1925.0,
    -1.0 / 16632.0,
]


def iota(shape, dim):
    return lax.broadcasted_iota(jnp.int32, shape, dim)


def band(distance):
    d = jnp.abs(distance)
    out = jnp.zeros(distance.shape, F32)
    for k in range(1, 7):
        out = jnp.where(d == k, -0.5 * COEFF[k], out)
    return out


def split3(v):
    hi = v.astype(jnp.bfloat16)
    left = v - hi.astype(F32)
    mid = left.astype(jnp.bfloat16)
    low = (left - mid.astype(F32)).astype(jnp.bfloat16)
    return hi, mid, low


def exact_dot(v, units, dims, flip=False):
    units = units.astype(jnp.bfloat16)
    total = None
    for term in reversed(split3(v)):
        pair = (units, term) if flip else (term, units)
        out = lax.dot_general(*pair, (dims, ((), ())), preferred_element_type=F32)
        total = out if total is None else total + out
    return total


def residues(n):
    return [0, 1] if n == 2 else [0, 1, n - 1]


def kernel(
    sizes,
    x_hbm, pot_hbm, p_hbm, cpl_hbm, st_hbm, cnt_hbm,
    out_hbm,
    base, xt, xe, ye, pot, pv, pr, sheared, accs, zs, zr, recv, zc, wrep, cs, mprime, fold,
    cpl_ref, st_ref, cnt_ref,
    lsem, hsend, hrecv, psend, precv,
):
    names = ("gx", "gy", "gz")
    me = [lax.axis_index(name) for name in names]
    res = [residues(n) for n in sizes]
    slots = {}
    for ex in res[0]:
        for ey in res[1]:
            for ez in res[2]:
                slots[(ex, ey, ez)] = len(slots)

    near_by = []
    for d in range(3):
        up = jnp.where(me[d] == sizes[d] - 1, 0, me[d] + 1)
        down = jnp.where(me[d] == 0, sizes[d] - 1, me[d] - 1)
        near_by.append({0: me[d], sizes[d] - 1: down, 1: up})

    def device(offset):
        return tuple(near_by[d][offset[d] % sizes[d]] for d in range(3))

    def slot_of(offset):
        return slots[tuple(offset[d] % sizes[d] for d in range(3))]

    load_x = pltpu.make_async_copy(x_hbm, xe.at[:, 6:22], lsem.at[0])
    load_y = pltpu.make_async_copy(x_hbm, ye.at[:, :, 8:24], lsem.at[1])
    load_p = [
        pltpu.make_async_copy(p_hbm.at[pl.ds(k * 2048, 2048)], pv.at[pl.ds(k * 2048, 2048)],
                              lsem.at[7 + k])
        for k in range(2)
    ]
    load_pot = pltpu.make_async_copy(pot_hbm, pot, lsem.at[3])
    load_st = pltpu.make_async_copy(st_hbm, st_ref, lsem.at[4])
    load_cnt = pltpu.make_async_copy(cnt_hbm, cnt_ref, lsem.at[5])
    load_cpl = pltpu.make_async_copy(cpl_hbm, cpl_ref, lsem.at[6])
    load_st.start()
    for copy in load_p:
        copy.start()
    load_x.start()
    load_cpl.start()
    load_cnt.start()
    load_y.start()
    load_pot.start()

    barrier = pltpu.get_barrier_semaphore()
    others = [e for e in slots if e != (0, 0, 0)]
    others.sort(key=lambda e: -sum(e))
    for e in others:
        pl.semaphore_signal(barrier, inc=1, device_id=device(e), device_id_type=MESH)

    def clear(i, carry):
        for b in range(2):
            xt[b, i] = jnp.zeros((48, 128), F32)
        return carry

    lax.fori_loop(0, 48, clear, 0)

    def clear_mix(i, carry):
        zc[pl.ds(i * 96, 96), :] = jnp.zeros((96, 128), F32)
        return carry

    lax.fori_loop(0, 24, clear_mix, 0)

    def clear_sum(i, carry):
        for b in range(2):
            sheared[b, i] = jnp.zeros((16, 128), F32)
        return carry

    lax.fori_loop(0, 16, clear_sum, 0)

    lane = iota((8, 128), 1)

    def place(o, s):
        a = st_ref[0, s, o] - 16 * (o >> 2)
        b0 = st_ref[1, s, o] - 16 * ((o >> 1) & 1)
        c = st_ref[2, s, o] - 128 * (o & 1)
        return a, b0, c

    load_x.wait()

    fold[...] = xe[:, 6:22].reshape(512, 128)
    for b in range(2):
        planes = [fold[pl.ds(b * 256 + y, 16, stride=16), :] for y in range(16)]
        planes = [pltpu.roll(v, 16 * (y % 8), 1) if y % 8 else v for y, v in enumerate(planes)]
        for y, v in enumerate(planes):
            xt[b, 16 + y, 16:32, :] = v

    row, col = iota((16, 128), 0), iota((16, 128), 1)
    sel = (col == jnp.where(row < 8, 120 + row, row - 8)).astype(F32)
    zs[...] = exact_dot(fold[...], sel, ((1,), (1,)), flip=True)
    pl.semaphore_wait(barrier, len(others))

    sends = []

    def send(src, dst, k, offset):
        copy = pltpu.make_async_remote_copy(
            src_ref=src, dst_ref=dst, send_sem=hsend.at[k], recv_sem=hrecv.at[k],
            device_id=device(offset), device_id_type=MESH,
        )
        copy.start()
        sends.append(copy)

    send(x_hbm.at[:, :, 8:16, :], ye.at[:, :, 0:8, :], 0, (0, 1, 0))
    send(x_hbm.at[:, :, 0:8, :], ye.at[:, :, 24:32, :], 1, (0, -1, 0))
    send(x_hbm.at[:, 10:16], xe.at[:, 0:6], 2, (1, 0, 0))
    send(x_hbm.at[:, 0:6], xe.at[:, 22:28], 3, (-1, 0, 0))
    send(zs.at[0:8], zr.at[0:8], 4, (0, 0, 1))
    send(zs.at[8:16], zr.at[8:16], 5, (0, 0, -1))

    load_st.wait()
    load_cnt.wait()

    def gather(n, carry):
        a, b0, c = place(n >> 2, n & 3)
        slabs = [
            xt[b, pl.ds(16 + b0, 16), pl.ds(16 + a, 16), :] for b in range(2)
        ]
        first = lane - 16 * b0
        parts = [(b, yh, h) for b in range(2) for yh in range(2) for h in range(2)]
        packed = {k: jnp.zeros((8, 128), F32) for k in parts}
        for y in range(8):
            z = (first - 16 * y) & 127
            keep = (z >= c) & (z < c + 16)
            for b, yh, h in parts:
                w = slabs[b][8 * yh + y, 8 * h : 8 * h + 8]
                packed[b, yh, h] = jnp.where(keep, w, packed[b, yh, h])
        by = (c + 16 * b0) & 127
        for i in range(4):
            acc = [None, None]
            for yh in range(2):
                plane = pltpu.roll(pv[pl.ds(n * 128 + yh * 4 + i, 16, stride=8), :], by, 1)
                pr[pl.ds(n * 128 + i * 32 + yh * 16, 16), :] = plane
                for b in range(2):
                    term = (packed[b, yh, 0] * plane[0:8]) + (packed[b, yh, 1] * plane[8:16])
                    acc[b] = term if acc[b] is None else acc[b] + term
            for b in range(2):
                accs[pl.ds(n * 64 + (b * 4 + i) * 8, 8), :] = acc[b]
        return carry

    for k in range(2):
        load_p[k].wait()
        lax.fori_loop(16 * k, 16 * k + 16, gather, 0, unroll=2)

    total = accs[pl.ds(0, 256, stride=8), :]
    for k in range(1, 8):
        total = total + accs[pl.ds(k, 256, stride=8), :]
    mine = exact_dot(total, jnp.ones((8, 128), F32), ((1,), (1,)), flip=True)
    recv[0] = mine[0:1]
    parts = []
    for k, e in enumerate(others):
        copy = pltpu.make_async_remote_copy(
            src_ref=recv.at[0], dst_ref=recv.at[slot_of(tuple(-v for v in e))],
            send_sem=psend.at[k], recv_sem=precv.at[slot_of(tuple(-v for v in e))],
            device_id=device(e), device_id_type=MESH,
        )
        copy.start()
        parts.append(copy)

    load_y.wait()
    load_pot.wait()
    r128, c128 = iota((128, 128), 0), iota((128, 128), 1)
    near = jnp.where(r128 == c128, -0.5 * 3.0 * COEFF[0], band(r128 - c128))
    base[...] = lax.dot_general(fold[...], near, (((1,), (0,)), ((), ())), precision=HI,
                           preferred_element_type=F32)
    for copy in sends[:4]:
        copy.wait_recv()

    def stencil(x, carry):
        done = []
        for b in range(2):
            here = pl.ds(b * 256 + x * 16, 16)
            acc = pot[x] * xe[b, x + 6] + base[here, :]
            for k in range(1, 7):
                four = (ye[b, x, 8 - k : 24 - k, :] + ye[b, x, 8 + k : 24 + k, :]) + (
                    xe[b, x + 6 - k] + xe[b, x + 6 + k]
                )
                acc = acc + (-0.5 * COEFF[k]) * four
            done.append(acc)
        for b in range(2):
            base[pl.ds(b * 256 + x * 16, 16), :] = done[b]
        return carry

    lax.fori_loop(0, 16, stencil, 0)

    load_cpl.wait()

    for s in range(4):
        for i in range(4):
            cs[pl.ds((s * 4 + i) * 4, 4), :] = cpl_ref[s, i]
    pick = (iota((8, 256), 0) == iota((8, 256), 1) // 32).astype(F32)
    spread = exact_dot(cs[...], pick, ((1,), (0,)))
    r64, c64 = iota((64, 256), 0), iota((64, 256), 1)
    own = (r64 // 16 == (c64 // 8) % 4) & (r64 % 4 == c64 % 4)
    spread = jnp.where(own, spread, 0.0)
    rows_of = (iota((8, 64), 0) % 4 == (iota((8, 64), 1) // 4) % 4).astype(F32)
    by_lane = exact_dot(spread, rows_of, ((1,), (0,)), flip=True)
    lane8 = iota((8, 256), 1)
    count = jnp.zeros((8, 256), jnp.int32)
    for o in range(8):
        count = jnp.where(lane8 // 32 == o, cnt_ref[o], count)
    mprime[...] = jnp.where((lane8 // 8) % 4 < count, by_lane, 0.0)

    for copy in sends[4:]:
        copy.wait_recv()
    far = band(jnp.where(row < 8, row - 8, 120 + row) - col)
    edge = lax.dot_general(zr[...], far, (((0,), (0,)), ((), ())), precision=HI,
                           preferred_element_type=F32)
    base[...] += edge


    for copy in parts:
        copy.wait_recv()

    def got(dx, dy, dz):
        r = recv[slot_of((dx, dy, dz))]
        return r[:, 0:128], r[:, 128:256]

    lane1 = iota((1, 128), 1)
    upper_y, upper_z = (lane1 & 64) != 0, (lane1 & 32) != 0
    halves = []
    for h in range(2):
        by_z = {}
        for dz in (-1, 0, 1):
            by_y = {}
            for dy in (-1, 0, 1):
                by_y[dy] = got(0, dy, dz)[h] + got(1 - 2 * h, dy, dz)[1 - h]
            crossed = jnp.where(upper_y, by_y[1], by_y[-1])
            by_z[dz] = by_y[0] + pltpu.roll(crossed, 64, 1)
        down = pltpu.roll(by_z[1], 96, 1)
        up = pltpu.roll(by_z[-1], 32, 1)
        halves.append(by_z[0] + jnp.where(upper_z, up, down))
    for h in range(2):
        v = mprime[:, 128 * h : 128 * h + 128] * halves[h]
        v = v + pltpu.roll(v, 127, 1)
        v = v + pltpu.roll(v, 126, 1)
        for g in range(32):
            wrep[(h * 32 + g) * 8 : (h * 32 + g) * 8 + 8, :] = jnp.broadcast_to(
                v[:, 4 * g : 4 * g + 1], (8, 128)
            )

    def scatter(o, carry):
        spots = []
        for s in range(4):
            n = o * 4 + s
            planes = pr[pl.ds(n * 128, 128), :]
            for b in range(2):
                mix = None
                for i in range(4):
                    term = planes[i * 32 : i * 32 + 32] * wrep[pl.ds(n * 16 + b * 8 + i, 1), :]
                    mix = term if mix is None else mix + term
                for yh in range(2):
                    at = (s * 12 + b * 6 + 2 + yh) * 48 + 16
                    zc[at : at + 16, :] = mix[yh * 16 : yh * 16 + 16]
            spots.append(place(o, s))
        for r in range(8):
            keep = []
            z = (lane - 16 * r) & 127
            for a, b0, c in spots:
                keep.append((z >= c) & (z < c + 16))
            corner = {
                (s, y): ((y - b0) >> 3) * 48 - a
                for s, (a, b0, c) in enumerate(spots) for y in (r, r + 8)
            }
            where = [(b, y, h) for y in (r, r + 8) for b in range(2) for h in range(2)]
            sums = []
            for b, y, h in where:
                acc = sheared[b, y, 8 * h : 8 * h + 8, :]
                for s in range(4):
                    at = (s * 12 + b * 6 + 2) * 48 + 16 + 8 * h
                    w = zc[pl.ds(corner[s, y] + at, 8), :]
                    acc = acc + jnp.where(keep[s], w, 0.0)
                sums.append(acc)
            for (b, y, h), acc in zip(where, sums):
                sheared[b, y, 8 * h : 8 * h + 8, :] = acc
        return carry

    lax.fori_loop(0, 8, scatter, 0)

    outs = []
    for b in range(2):
        planes = [sheared[b, y] for y in range(16)]
        planes = [
            (pltpu.roll(v, 128 - 16 * (y % 8), 1) if y % 8 else v)
            + base[pl.ds(b * 256 + y, 16, stride=16), :]
            for y, v in enumerate(planes)
        ]
        for y, v in enumerate(planes):
            base[pl.ds(b * 256 + y, 16, stride=16), :] = v
        half = pl.ds(b * 256, 256)
        outs.append(pltpu.make_async_copy(base.at[half], out_hbm.at[half], lsem.at[11 + b]))
        outs[b].start()
    for copy in sends + parts:
        copy.wait_send()
    for copy in outs:
        copy.wait()


def solution(mesh):
    sizes = tuple(mesh.shape[name] for name in ("gx", "gy", "gz"))
    nslots = 1
    for n in sizes:
        nslots *= len(residues(n))

    def on_device(orbitals, potential, projectors, coupling, block_starts, owner_counts):
        rows = projectors.reshape(32, 4, 32, 128).transpose(0, 2, 1, 3).reshape(4096, 128)
        matrices = coupling.reshape(8, 4, 4, 4).transpose(1, 2, 3, 0)
        starts = block_starts.reshape(8, 4, 3).transpose(2, 1, 0)
        counts = owner_counts.reshape(8)
        hbm = pl.BlockSpec(memory_space=pltpu.HBM)
        return pl.pallas_call(
            functools.partial(kernel, sizes),
            out_shape=jax.ShapeDtypeStruct((512, 128), F32),
            in_specs=[hbm] * 6,
            out_specs=hbm,
            scratch_shapes=[
                pltpu.VMEM((512, 128), F32),
                pltpu.VMEM((2, 48, 48, 128), F32),
                pltpu.VMEM((2, 28, 16, 128), F32),
                pltpu.VMEM((2, 16, 32, 128), F32),
                pltpu.VMEM((16, 16, 128), F32),
                pltpu.VMEM((4096, 128), F32),
                pltpu.VMEM((4096, 128), F32),
                pltpu.VMEM((2, 16, 16, 128), F32),
                pltpu.VMEM((2048, 128), F32),
                pltpu.VMEM((16, 512), F32),
                pltpu.VMEM((16, 512), F32),
                pltpu.VMEM((nslots, 1, 256), F32),
                pltpu.VMEM((2304, 128), F32),
                pltpu.VMEM((512, 128), F32),
                pltpu.VMEM((64, 8), F32),
                pltpu.VMEM((8, 256), F32),
                pltpu.VMEM((512, 128), F32),
                pltpu.VMEM((4, 4, 4, 8), F32),
                pltpu.SMEM((3, 4, 8), jnp.int32),
                pltpu.SMEM((8,), jnp.int32),
                pltpu.SemaphoreType.DMA((13,)),
                pltpu.SemaphoreType.DMA((6,)),
                pltpu.SemaphoreType.DMA((6,)),
                pltpu.SemaphoreType.DMA((nslots,)),
                pltpu.SemaphoreType.DMA((nslots,)),
            ],
            compiler_params=pltpu.CompilerParams(
                collective_id=0, has_side_effects=True, vmem_limit_bytes=60 * 1024 * 1024
            ),
        )(orbitals, potential, rows, matrices, starts, counts).reshape(2, 16, 16, 128)

    in_specs = (
        P(None, "gx", "gy", "gz"),
        P("gx", "gy", "gz"),
        P("gx", "gy", "gz", None, None, None, None),
        P("gx", "gy", "gz", None, None, None, None),
        P("gx", "gy", "gz", None, None, None),
        P("gx", "gy", "gz", None),
    )
    return jax.shard_map(
        on_device, mesh=mesh, in_specs=in_specs,
        out_specs=P(None, "gx", "gy", "gz"), check_vma=False,
    )
```
